512 devices in a mesh: seq: 64 (over z, x, core), dp: 8 (over y).
Axes of the slice: x: 4, y: 8, z: 8, core: 2. Of those that a mesh axis runs over, the one named last changes fastest.
Arguments:
- tokens: bfloat16 [8, 16384, 256], P('dp', 'seq'), may hold values from -6 to 6
- occupancy: int32 [8, 16384], P('dp', 'seq'), may hold values 0 or 1
- counts: int32 [8, 64], P('dp', 'seq'), may hold values from 64 to 256, as said below
- queries: bfloat16 [512, 1024], replicated, may hold values from -6 to 6
- saved_lse: float32 [8, 512, 8], P('dp', 'seq'), as said below
- grad_out: bfloat16 [8, 512, 1024], P('dp', 'seq'), may hold values from -6 to 6
- attn_out: bfloat16 [8, 512, 1024], P('dp', 'seq'), may hold values from -6 to 6
- w_key: bfloat16 [256, 1024], replicated, may hold values from -0.375 to 0.375
- w_value: bfloat16 [256, 1024], replicated, may hold values from -0.375 to 0.375
Outputs:
- grad_tokens: bfloat16 [8, 16384, 256], P('dp', 'seq')
- grad_queries: float32 [512, 1024], P('seq')
- grad_w_key: float32 [256, 1024], replicated
- grad_w_value: float32 [256, 1024], replicated
The draws below stay inside these ranges and needn't reach their ends.
Inputs may be any that keep to these rules, and one draw needn't show every extreme that they name: `counts`: each shard's count lies between 64 and 256; in every draw some shard is full. `saved_lse`: values lie near the logarithm of a window's number of occupied tokens.
All inputs are finite; a program needn't handle non-finite values. No bound on the sum of `occupancy` on one device may be relied on, other than what follows from the above.
Results may differ from the reference program's by a relative error of at most 0.0082.
The reference program's roundings to bfloat16 on the way (of `normal`, `probs_low`, `grad_values`, `grad_scores` and `grad_keys`) count: a program that leaves them out, or rounds other values in their place, can miss the bound.
Values may be sent and summed in bfloat16 or wider, within the bound.
No kernel may reach another device: no remote copies, remote signals or barrier semaphores. Data moves between devices by JAX's collectives and lax.ppermute only.
A program may use at most 64 MiB of HBM per device.

```python
import math
import jax
import jax.numpy as jnp
from jax import lax

DT = 256
LATENTS = 512
HEADS = 8
TOK_DEV = 256
INNER = 1024
TOKENS = 16384
WINDOWS = 8
SHARDS = 64


def draw_counts(key, part):
    key = jax.random.fold_in(key, 5)
    first, second = jax.random.split(key)
    drawn = jax.random.randint(first, (WINDOWS * SHARDS,), TOK_DEV // 4, TOK_DEV + 1, dtype=jnp.int32)
    chosen = jax.random.randint(second, (), 0, WINDOWS * SHARDS, dtype=jnp.int32)
    filled = jnp.where(jnp.arange(WINDOWS * SHARDS, dtype=jnp.int32) == chosen, TOK_DEV, drawn)
    return filled.reshape(WINDOWS, SHARDS).astype(jnp.int32)


def draw_saved_lse(key, part):
    key = jax.random.fold_in(key, 9)
    center = math.log(TOKENS * 0.45) + 0.5
    offset = jax.random.uniform(key, (WINDOWS, LATENTS, HEADS), jnp.float32, -0.5, 0.5)
    return (center + offset).astype(jnp.float32)


def touch_ends(values, key, least, top_value):
    longest = values.shape.index(max(values.shape))
    spots = []
    for shift in (0, 1):
        where = [jax.random.randint(jax.random.fold_in(key, axis), (), 0, length) for axis, length in enumerate(values.shape)]
        where[longest] = (where[longest] + shift) % values.shape[longest]
        spots.append(tuple(where))
    return values.at[spots[0]].set(least).at[spots[1]].set(top_value)


def shard_levels(own_key, dims, cuts, smallest, largest):
    level, own = 1.0, jax.random.fold_in(own_key, 6)
    for axis_at, shards_of in cuts:
        heights = jnp.exp(jax.random.uniform(jax.random.fold_in(own, axis_at), (shards_of,), jnp.float32, smallest / len(cuts), largest / len(cuts)))
        level = level * jnp.repeat(heights, dims[axis_at] // shards_of).reshape([-1 if axis == axis_at else 1 for axis in range(len(dims))])
    return level


def noise(own_key, extent, scale, most, shards=(), kind=jnp.bfloat16):
    entries = jax.random.normal(own_key, extent, jnp.float32) * scale
    if len(shards) > 0:
        entries = shard_levels(own_key, extent, shards, -0.22, 0.18) * entries
    return jnp.clip(entries, min=-most, max=most).astype(kind)


def setup_inputs(seed: int = 0) -> dict:
    splits = jax.random.split(jax.random.key(seed), 10)
    return {
        "tokens": noise(splits[0], (WINDOWS, TOKENS, DT), 1.0, 6.0, ((0, 8), (1, 64))),
        "occupancy": touch_ends((jax.random.randint(splits[1], (WINDOWS, TOKENS), 0, 4) < 3).astype(jnp.int32), jax.random.fold_in(splits[1], 1), 0, 1),
        "counts": draw_counts(jax.random.fold_in(splits[9], 71), 0),
        "queries": noise(splits[3], (LATENTS, INNER), 1.0, 6.0),
        "saved_lse": draw_saved_lse(jax.random.fold_in(splits[9], 71), 0),
        "grad_out": noise(splits[5], (WINDOWS, LATENTS, INNER), 1.0, 6.0, ((0, 8), (1, 64))),
        "attn_out": noise(splits[6], (WINDOWS, LATENTS, INNER), 0.5, 6.0, ((0, 8), (1, 64))),
        "w_key": noise(splits[7], (DT, INNER), DT ** -0.5, 0.375),
        "w_value": noise(splits[8], (DT, INNER), DT ** -0.5, 0.375),
    }


def layer_norm(tokens_f32):
    center = tokens_f32 - lax.optimization_barrier(jnp.mean(tokens_f32, axis=-1, keepdims=True))
    inverse = lax.rsqrt(lax.optimization_barrier(jnp.mean(center * center, axis=-1, keepdims=True)) + 1e-05)
    return (center * inverse, inverse)

def split_heads(matrix, heads):
    return matrix.reshape(matrix.shape[0], heads, -1).transpose(1, 0, 2)

def join_heads(stacked):
    return stacked.transpose(1, 0, 2).reshape(stacked.shape[1], -1)

def head_sums(grad_rows, out_rows, heads):
    product = grad_rows.astype(jnp.float32) * out_rows.astype(jnp.float32)
    return lax.optimization_barrier(jnp.sum(product.reshape(product.shape[0], heads, -1), axis=-1))

def head_backward(live_keys, scale_factor):

    def one_head(carry, items):
        query_head, key_head, value_head, grad_head, lse_head, delta_head = items
        scores = lax.dot_general(query_head, key_head, (((1,), (1,)), ((), ())), preferred_element_type=jnp.float32) * scale_factor
        probs = live_keys[None, :] * jnp.exp(scores - lse_head[:, None])
        probs_low = probs.astype(jnp.bfloat16)
        grad_value = lax.dot_general(probs_low, grad_head, (((0,), (0,)), ((), ())), preferred_element_type=jnp.float32).astype(jnp.bfloat16)
        grad_probs = lax.dot_general(grad_head, value_head, (((1,), (1,)), ((), ())), preferred_element_type=jnp.float32)
        grad_scores = (scale_factor * probs * (grad_probs - delta_head[:, None])).astype(jnp.bfloat16)
        grad_query = jnp.dot(grad_scores, key_head, preferred_element_type=jnp.float32)
        grad_key = lax.dot_general(grad_scores, query_head, (((0,), (0,)), ((), ())), preferred_element_type=jnp.float32).astype(jnp.bfloat16)
        return (carry, (grad_query, grad_key, grad_value))
    return one_head

def window_backward(tokens_window, live_keys, queries, lse_rows, delta_rows, grad_rows, w_key, w_value):
    heads = lse_rows.shape[1]
    scale_factor = 1.0 / math.sqrt(queries.shape[1] // heads)
    normal_f32, inverse = layer_norm(tokens_window.astype(jnp.float32))
    normal_low = normal_f32.astype(jnp.bfloat16)
    key_rows = jnp.dot(normal_low, w_key, preferred_element_type=jnp.float32).astype(jnp.bfloat16)
    value_rows = jnp.dot(normal_low, w_value, preferred_element_type=jnp.float32).astype(jnp.bfloat16)
    items = (split_heads(queries, heads), split_heads(key_rows, heads), split_heads(value_rows, heads), split_heads(grad_rows, heads), lse_rows.T, delta_rows.T)
    _, stacked = lax.scan(head_backward(live_keys, scale_factor), jnp.zeros((), jnp.float32), items)
    grad_query = join_heads(stacked[0])
    grad_keys = join_heads(stacked[1])
    grad_values = join_heads(stacked[2])
    grad_wkey = lax.dot_general(normal_low, grad_keys, (((0,), (0,)), ((), ())), preferred_element_type=jnp.float32)
    grad_wvalue = lax.dot_general(normal_low, grad_values, (((0,), (0,)), ((), ())), preferred_element_type=jnp.float32)
    grad_normal = lax.dot_general(grad_keys, w_key, (((1,), (1,)), ((), ())), preferred_element_type=jnp.float32)
    grad_normal = grad_normal + lax.dot_general(grad_values, w_value, (((1,), (1,)), ((), ())), preferred_element_type=jnp.float32)
    grad_input = inverse * (grad_normal - lax.optimization_barrier(jnp.mean(grad_normal, axis=-1, keepdims=True)) - normal_f32 * lax.optimization_barrier(jnp.mean(grad_normal * normal_f32, axis=-1, keepdims=True)))
    return (grad_input.astype(jnp.bfloat16), grad_query, grad_wkey, grad_wvalue)

def reference(tokens, occupancy, counts, queries, saved_lse, grad_out, attn_out, w_key, w_value):
    heads = saved_lse.shape[2]

    def per_window(index_window):
        count_rows = jnp.repeat(counts[index_window], TOK_DEV, total_repeat_length=TOKENS)
        positions = (jnp.arange(TOKENS, dtype=jnp.int32) % TOK_DEV).astype(jnp.int32)
        live_keys = jnp.where(positions < count_rows, occupancy[index_window], 0).astype(jnp.float32)
        delta_rows = head_sums(grad_out[index_window], attn_out[index_window], heads)
        return window_backward(tokens[index_window], live_keys, queries, saved_lse[index_window], delta_rows, grad_out[index_window], w_key, w_value)
    results = lax.map(per_window, jnp.arange(WINDOWS, dtype=jnp.int32))
    return (results[0], lax.optimization_barrier(jnp.sum(results[1], axis=0)), lax.optimization_barrier(jnp.sum(results[2], axis=0)), lax.optimization_barrier(jnp.sum(results[3], axis=0)))
```

```python
import math

import jax
import jax.numpy as jnp
from jax import lax
from jax.experimental import pallas as pl
from jax.experimental.pallas import tpu as pltpu
from jax.sharding import Mesh
from jax.sharding import PartitionSpec as P

HEAD = 128
EPS = 1e-05
LOG2E = math.log2(math.e)
PAD = 16
F32, BF16 = jnp.float32, jnp.bfloat16
VMEM = pl.BlockSpec(memory_space=pltpu.VMEM)
SMEM = pl.BlockSpec(memory_space=pltpu.SMEM)


def params(mib):
    return pltpu.CompilerParams(vmem_limit_bytes=mib * 1024 * 1024)


def mm(left, right, left_dim, right_dim):
    return lax.dot_general(
        left, right, (((left_dim,), (right_dim,)), ((), ())), preferred_element_type=F32
    )


def layer_norm(tokens):
    center = tokens - jnp.mean(tokens, axis=-1, keepdims=True)
    inverse = lax.rsqrt(jnp.mean(center * center, axis=-1, keepdims=True) + EPS)
    return center * inverse, inverse


def live_rows(occupancy, count, width):
    shard = occupancy.shape[1]
    place = lax.broadcasted_iota(jnp.int32, (1, shard), 1)
    live = jnp.where(place < count, occupancy, 0).astype(F32)
    return jnp.broadcast_to(live, (width, shard)).T


def three_parts(column):
    parts = []
    for _ in range(3):
        part = column.astype(BF16).astype(F32)
        parts.append(part)
        column = column - part
    return parts


def pack_kernel(counts, tokens, occupancy, grad, out, lse, sent):
    heads, (shard, width) = sent.shape[0], tokens.shape
    live = live_rows(occupancy[...], counts[0, 0], width)
    masked = jnp.where(live > 0.0, tokens[...].astype(F32), 0.0).astype(BF16)
    rows = grad.shape[0]
    lane = lax.broadcasted_iota(jnp.int32, (rows, HEAD), 1)
    for head in range(heads):
        sent[head, :shard, :] = masked
        cols = slice(head * HEAD, (head + 1) * HEAD)
        grad_f32 = grad[:, cols].astype(F32)
        delta = jnp.sum(grad_f32 * out[:, cols].astype(F32), axis=1, keepdims=True)
        extra = jnp.zeros((rows, HEAD), F32)
        for at, part in enumerate(three_parts(lse[:, head : head + 1]) + three_parts(delta)):
            extra = jnp.where(lane == at, part, extra)
        both = jnp.concatenate([grad_f32, extra], axis=1)
        both = jnp.concatenate([both, jnp.zeros((PAD - rows, 2 * HEAD), F32)], axis=0)
        sent[head, shard:, :] = both.astype(BF16)


def main_kernel(head, got, rows, query, w_key, w_value, back, parts, query_sum, weight_sum):
    del head
    blocks, shard = back.shape[0], back.shape[1]
    groups, part_rows = parts.shape[0], parts.shape[1]
    scale = 1.0 / math.sqrt(HEAD)
    grad = rows[:, :HEAD]
    extra = rows[:, HEAD:].astype(F32).T
    lse = (extra[0:1] + extra[1:2] + extra[2:3]) * LOG2E
    delta = extra[3:4] + extra[4:5] + extra[5:6]
    queries = query[...]
    weights = jnp.concatenate([w_key[...], w_value[...]], axis=1)
    for block in range(blocks):
        normal = layer_norm(got[block, :shard, :].astype(F32))[0].astype(BF16)
        both = jnp.dot(normal, weights, preferred_element_type=F32).astype(BF16)
        keys, values = both[:, :HEAD], both[:, HEAD:]
        probs = jnp.exp2(mm(keys, queries, 1, 1) * (scale * LOG2E) - lse)
        grad_values = jnp.dot(probs.astype(BF16), grad, preferred_element_type=F32)
        grad_probs = mm(values, grad, 1, 1)
        grad_scores = (scale * probs * (grad_probs - delta)).astype(BF16)
        grad_keys = jnp.dot(grad_scores, queries, preferred_element_type=F32)
        grad_both = jnp.concatenate([grad_keys, grad_values], axis=1).astype(BF16)
        back[block] = grad_both
        query_part = mm(keys, grad_scores, 0, 0)
        weight_part = mm(normal, grad_both, 0, 0)
        if block == 0:
            query_sum[...] = query_part
            weight_sum[...] = weight_part
        else:
            query_sum[...] += query_part
            weight_sum[...] += weight_part
    turned = query_sum[...].T.astype(BF16)
    totals = weight_sum[...].astype(BF16)
    each = weight_sum.shape[0] // groups
    half = part_rows - each
    for group in range(groups):
        parts[group, :each, :] = totals[group * each : (group + 1) * each, :]
        start = group * 2 * half
        parts[group, each:, :HEAD] = turned[start : start + half]
        parts[group, each:, HEAD:] = turned[start + half : start + 2 * half]


def add_up(got):
    total = got[0].astype(F32)
    for at in range(1, got.shape[0]):
        total = total + got[at].astype(F32)
    return total


def spread_kernel(got, sent):
    total = add_up(got).astype(BF16)
    for at in range(sent.shape[0]):
        sent[at] = total


def total_kernel(got, sent, query_rows):
    total = add_up(got)
    each = sent.shape[1]
    low = total[:each].astype(BF16)
    for at in range(sent.shape[0]):
        sent[at] = low
    query_rows[: got.shape[1] - each, :] = total[each:, :HEAD]
    query_rows[got.shape[1] - each :, :] = total[each:, HEAD:]


def gather_kernel(back, weights, query_rows, sent):
    blocks, shard = back.shape[0], back.shape[1]
    depth = weights.shape[0]
    rows = query_rows.shape[0] // blocks
    for block in range(blocks):
        sent[block, :shard, :] = back[block]
        sent[block, shard : shard + depth, :] = weights[...]
        piece = query_rows[block * rows : (block + 1) * rows, :]
        high = piece.astype(BF16).astype(F32)
        both = jnp.concatenate([high, piece - high], axis=1)
        both = jnp.concatenate([both, jnp.zeros((PAD - rows, 2 * HEAD), F32)], axis=0)
        sent[block, shard + depth :, :] = both.astype(BF16)


def finish_kernel(
    counts, got, tokens, occupancy, w_key, w_value, grad_tokens, query_rows, key_total, value_total
):
    heads, (shard, width) = got.shape[0], tokens.shape
    depth = key_total.shape[0]
    rows = query_rows.shape[0]
    normal, inverse = layer_norm(tokens[...].astype(F32))
    grad_normal = jnp.zeros((shard, width), F32)
    for head in range(heads):
        cols = slice(head * HEAD, (head + 1) * HEAD)
        weights = jnp.concatenate([w_key[:, cols], w_value[:, cols]], axis=1)
        grad_normal += mm(got[head, :shard, :], weights, 1, 1)
        both = got[head, shard : shard + depth, :].astype(F32)
        key_total[:, cols] = both[:, :HEAD]
        value_total[:, cols] = both[:, HEAD:]
        piece = got[head, shard + depth :, :].astype(F32)
        query_rows[:, cols] = (piece[:, :HEAD] + piece[:, HEAD:])[:rows]
    live = live_rows(occupancy[...], counts[0, 0], width)
    grad_normal = jnp.where(live > 0.0, grad_normal, 0.0)
    grad_input = inverse * (
        grad_normal
        - jnp.mean(grad_normal, axis=-1, keepdims=True)
        - normal * jnp.mean(grad_normal * normal, axis=-1, keepdims=True)
    )
    grad_tokens[...] = grad_input.astype(BF16)


def swap(array, axis):
    return lax.all_to_all(array, axis, 0, 0, tiled=True)


def shape(dims, dtype=BF16):
    return jax.ShapeDtypeStruct(dims, dtype)


def body(tokens, occupancy, counts, queries, saved_lse, grad_out, attn_out, w_key, w_value):
    tokens, grad, out, lse = tokens[0], grad_out[0], attn_out[0], saved_lse[0]
    heads, (shard, width) = lse.shape[1], tokens.shape
    latents, rows = queries.shape[0], grad.shape[0]
    groups = latents // (rows * heads)
    windows = lax.axis_size("y")
    sent = pl.pallas_call(
        pack_kernel,
        out_shape=shape((heads, shard + PAD, width)),
        in_specs=[SMEM] + [VMEM] * 5,
        out_specs=VMEM,
        compiler_params=params(16),
    )(counts, tokens, occupancy, grad, out, lse)
    got = swap(sent, "g")
    mine = got[:, shard : shard + rows, :].reshape(1, rows * heads, width)
    all_rows = swap(jnp.broadcast_to(mine, (groups, rows * heads, width)), "z")

    each, half = width // groups, rows * heads // 2
    head = lax.axis_index("g").reshape(1).astype(jnp.int32)
    whole3 = lambda at, head: (0, 0, 0)
    whole2 = lambda at, head: (0, 0)
    column = lambda at, head: (0, head[0])
    back, parts = pl.pallas_call(
        main_kernel,
        out_shape=(shape((heads, shard, width)), shape((groups, each + half, width))),
        grid_spec=pltpu.PrefetchScalarGridSpec(
            num_scalar_prefetch=1,
            grid=(1,),
            in_specs=[
                pl.BlockSpec(got.shape, whole3),
                pl.BlockSpec((latents, width), whole2),
                pl.BlockSpec((latents, HEAD), column),
                pl.BlockSpec((width, HEAD), column),
                pl.BlockSpec((width, HEAD), column),
            ],
            out_specs=[
                pl.BlockSpec((heads, shard, width), whole3),
                pl.BlockSpec((groups, each + half, width), whole3),
            ],
            scratch_shapes=[pltpu.VMEM((HEAD, latents), F32), pltpu.VMEM((width, width), F32)],
        ),
        compiler_params=params(40),
    )(head, got, all_rows.reshape(latents, width), queries, w_key, w_value)

    parts = swap(parts, "z")
    parts = pl.pallas_call(
        spread_kernel,
        out_shape=shape((windows, each + half, width)),
        in_specs=[VMEM],
        out_specs=VMEM,
        compiler_params=params(8),
    )(parts)
    parts = swap(parts, "y")
    weights, query_part = pl.pallas_call(
        total_kernel,
        out_shape=(shape((groups, each, width)), shape((2 * half, HEAD), F32)),
        in_specs=[VMEM],
        out_specs=(VMEM, VMEM),
        compiler_params=params(8),
    )(parts)
    weights = swap(weights, "z").reshape(width, width)
    sent = pl.pallas_call(
        gather_kernel,
        out_shape=shape((heads, shard + width + PAD, width)),
        in_specs=[VMEM] * 3,
        out_specs=VMEM,
        compiler_params=params(16),
    )(back, weights, query_part)
    got = swap(sent, "g")
    grad_tokens, query_rows, key_total, value_total = pl.pallas_call(
        finish_kernel,
        out_shape=(
            shape((shard, width)),
            shape((rows, heads * HEAD), F32),
            shape((width, heads * HEAD), F32),
            shape((width, heads * HEAD), F32),
        ),
        in_specs=[SMEM] + [VMEM] * 5,
        out_specs=(VMEM,) * 4,
        compiler_params=params(24),
    )(counts, got, tokens, occupancy, w_key, w_value)
    return grad_tokens[None], query_rows, key_total, value_total


def solution(mesh):
    seq, dp = mesh.shape["seq"], mesh.shape["dp"]
    split = Mesh(mesh.devices.reshape(seq // 8, 8, dp), ("z", "g", "y"))
    both = ("z", "g")
    rows = P("y", both, None)
    return jax.shard_map(
        body,
        mesh=split,
        in_specs=(rows, P("y", both), P("y", both), P(), rows, rows, rows, P(), P()),
        out_specs=(rows, P(both, None), P(), P()),
        check_vma=False,
    )
```

```python
import math

import jax
import jax.numpy as jnp
from jax import lax
from jax.experimental import pallas as pl
from jax.experimental.pallas import tpu as pltpu
from jax.sharding import Mesh
from jax.sharding import PartitionSpec as P

HEAD = 128
EPS = 1e-05
LOG2E = math.log2(math.e)
F32, BF16 = jnp.float32, jnp.bfloat16
VMEM = pl.BlockSpec(memory_space=pltpu.VMEM)
SMEM = pl.BlockSpec(memory_space=pltpu.SMEM)


def params(mib):
    return pltpu.CompilerParams(vmem_limit_bytes=mib * 1024 * 1024)


def mm(left, right, left_dim, right_dim):
    return lax.dot_general(
        left, right, (((left_dim,), (right_dim,)), ((), ())), preferred_element_type=F32
    )


def layer_norm(tokens):
    center = tokens - jnp.mean(tokens, axis=-1, keepdims=True)
    inverse = lax.rsqrt(jnp.mean(center * center, axis=-1, keepdims=True) + EPS)
    return center * inverse, inverse


def live_rows(occupancy, count, width):
    shard = occupancy.shape[1]
    place = lax.broadcasted_iota(jnp.int32, (1, shard), 1)
    live = jnp.where(place < count, occupancy, 0).astype(F32)
    return jnp.broadcast_to(live, (width, shard)).T


def three_parts(column):
    parts = []
    for _ in range(3):
        part = column.astype(BF16).astype(F32)
        parts.append(part)
        column = column - part
    return parts


def pack_kernel(*refs):
    sources, sent, (counts, tokens, occupancy, grad, out, lse), done = (
        refs[:6],
        refs[6],
        refs[7:13],
        refs[13],
    )
    copies = [
        pltpu.make_async_copy(source, target, done.at[at])
        for at, (source, target) in enumerate(zip(sources, refs[7:13]))
    ]
    for copy in copies:
        copy.start()
    for copy in copies:
        copy.wait()
    chips, (shard, width) = sent.shape[0], tokens.shape
    live = live_rows(occupancy[...], counts[0, 0], width)
    masked = jnp.where(live > 0.0, tokens[...].astype(F32), 0.0).astype(BF16)
    rows = grad.shape[0]
    lane = lax.broadcasted_iota(jnp.int32, (rows, HEAD), 1)
    for chip in range(chips):
        sent[chip, :shard, :] = masked
        extras, grads = [], []
        for head in (2 * chip, 2 * chip + 1):
            cols = slice(head * HEAD, (head + 1) * HEAD)
            grad_f32 = grad[:, cols].astype(F32)
            delta = jnp.sum(grad_f32 * out[:, cols].astype(F32), axis=1, keepdims=True)
            extra = jnp.zeros((rows, HEAD), F32)
            for at, part in enumerate(three_parts(lse[:, head : head + 1]) + three_parts(delta)):
                extra = jnp.where(lane == at, part, extra)
            extras.append(extra)
            grads.append(grad_f32)
        both = jnp.concatenate(
            [jnp.concatenate(grads, axis=1), jnp.concatenate(extras, axis=1)], axis=0
        )
        sent[chip, shard:, :] = both.astype(BF16)


def turn_kernel(got, sent):
    chips, width = got.shape[0], got.shape[2]
    shard = got.shape[1] - sent.shape[1] // chips * 2
    pieces = [got[chip, shard:, :].astype(F32) for chip in range(chips)]
    rows = sent.shape[1] // chips
    grads = jnp.concatenate([piece[:rows] for piece in pieces], axis=0)
    extras = jnp.concatenate([piece[rows:] for piece in pieces], axis=0)
    for core in range(2):
        cols = slice(core * HEAD, (core + 1) * HEAD)
        both = jnp.concatenate([grads[:, cols], extras[:, cols]], axis=1).astype(BF16)
        for group in range(sent.shape[0] // 2):
            sent[2 * group + core] = both


def latent_order(got, chips):
    rows = got.shape[1] // chips
    blocks = [got[at].astype(F32) for at in range(got.shape[0])]
    return jnp.concatenate(
        [
            blocks[2 * group + core][chip * rows : (chip + 1) * rows]
            for group in range(got.shape[0] // 2)
            for chip in range(chips)
            for core in range(2)
        ],
        axis=0,
    )


def main_kernel(
    head, mine, other, got, query, w_key, w_value, keep, give, parts, query_sum, weight_sum
):
    del head
    chips, shard = keep.shape[0], keep.shape[1]
    groups, part_rows = parts.shape[0], parts.shape[1]
    scale = 1.0 / math.sqrt(HEAD)
    rows = latent_order(got, chips)
    grad = rows[:, :HEAD].astype(BF16)
    extra = rows[:, HEAD:].T
    lse = (extra[0:1] + extra[1:2] + extra[2:3]) * LOG2E
    delta = extra[3:4] + extra[4:5] + extra[5:6]
    queries = query[...]
    weights = jnp.concatenate([w_key[...], w_value[...]], axis=1)
    for block in range(2 * chips):
        source, target = (mine, keep) if block < chips else (other, give)
        chip = block % chips
        normal = layer_norm(source[chip, :shard, :].astype(F32))[0].astype(BF16)
        both = jnp.dot(normal, weights, preferred_element_type=F32).astype(BF16)
        keys, values = both[:, :HEAD], both[:, HEAD:]
        probs = jnp.exp2(mm(keys, queries, 1, 1) * (scale * LOG2E) - lse)
        grad_values = jnp.dot(probs.astype(BF16), grad, preferred_element_type=F32)
        grad_probs = mm(values, grad, 1, 1)
        grad_scores = (scale * probs * (grad_probs - delta)).astype(BF16)
        grad_keys = jnp.dot(grad_scores, queries, preferred_element_type=F32)
        grad_both = jnp.concatenate([grad_keys, grad_values], axis=1).astype(BF16)
        target[chip] = grad_both
        query_part = mm(keys, grad_scores, 0, 0)
        weight_part = mm(normal, grad_both, 0, 0)
        if block == 0:
            query_sum[...] = query_part
            weight_sum[...] = weight_part
        else:
            query_sum[...] += query_part
            weight_sum[...] += weight_part
    turned = query_sum[...].T.astype(BF16)
    totals = weight_sum[...].astype(BF16)
    each = weight_sum.shape[0] // groups
    half = part_rows - each
    for group in range(groups):
        parts[group, :each, :] = totals[group * each : (group + 1) * each, :]
        start = group * 2 * half
        parts[group, each:, :HEAD] = turned[start : start + half]
        parts[group, each:, HEAD:] = turned[start + half : start + 2 * half]


def add_up(got):
    total = got[0].astype(F32)
    for at in range(1, got.shape[0]):
        total = total + got[at].astype(F32)
    return total


def spread_kernel(got, sent):
    total = add_up(got).astype(BF16)
    for at in range(sent.shape[0]):
        sent[at] = total


def total_kernel(got, sent, query_rows):
    total = add_up(got)
    each = sent.shape[1]
    low = total[:each].astype(BF16)
    for at in range(sent.shape[0]):
        sent[at] = low
    query_rows[: got.shape[1] - each, :] = total[each:, :HEAD]
    query_rows[got.shape[1] - each :, :] = total[each:, HEAD:]


def gather_kernel(
    heads, keep, theirs, weights, query_rows, my_key, my_value, their_key, their_value, sent
):
    del heads
    chips, shard = keep.shape[0], keep.shape[1]
    depth = weights.shape[0]
    rows = query_rows.shape[0] // chips
    mine = jnp.concatenate([my_key[...], my_value[...]], axis=1)
    other = jnp.concatenate([their_key[...], their_value[...]], axis=1)
    for chip in range(chips):
        grad_normal = mm(keep[chip], mine, 1, 1) + mm(theirs[chip], other, 1, 1)
        sent[chip, :shard, :] = grad_normal.astype(BF16)
        sent[chip, shard : shard + depth, :] = weights[...]
        piece = query_rows[chip * rows : (chip + 1) * rows, :]
        high = piece.astype(BF16).astype(F32)
        sent[chip, shard + depth :, :] = jnp.concatenate([high, piece - high], axis=1).astype(BF16)


def tokens_kernel(counts, got, tokens, occupancy, grad_tokens):
    chips, (shard, width) = got.shape[0], tokens.shape
    normal, inverse = layer_norm(tokens[...].astype(F32))
    grad_normal = got[0, :shard, :].astype(F32)
    for chip in range(1, chips):
        grad_normal += got[chip, :shard, :].astype(F32)
    live = live_rows(occupancy[...], counts[0, 0], width)
    grad_normal = jnp.where(live > 0.0, grad_normal, 0.0)
    grad_input = inverse * (
        grad_normal
        - jnp.mean(grad_normal, axis=-1, keepdims=True)
        - normal * jnp.mean(grad_normal * normal, axis=-1, keepdims=True)
    )
    grad_tokens[...] = grad_input.astype(BF16)


def finish_kernel(core, got, other, query_rows, key_total, value_total):
    chips, depth, rows = got.shape[0], key_total.shape[0], query_rows.shape[0]
    shard = got.shape[1] - depth - 2 * rows

    def write(low, high):
        for chip in range(chips):
            for at, source in ((2 * chip, low), (2 * chip + 1, high)):
                cols = slice(at * HEAD, (at + 1) * HEAD)
                both = source[chip, shard : shard + depth, :].astype(F32)
                key_total[:, cols] = both[:, :HEAD]
                value_total[:, cols] = both[:, HEAD:]
                piece = source[chip, shard + depth :, :].astype(F32)
                both_rows = piece[:, :HEAD] + piece[:, HEAD:]
                query_rows[:, cols] = jnp.where(core[0] == 0, both_rows[:rows], both_rows[rows:])

    @pl.when(core[0] == 0)
    def _():
        write(got, other)

    @pl.when(core[0] != 0)
    def _():
        write(other, got)


def swap(array, axis):
    return lax.all_to_all(array, axis, 0, 0, tiled=True)


def shape(dims, dtype=BF16):
    return jax.ShapeDtypeStruct(dims, dtype)


def sibling(array):
    return lax.ppermute(array, "c", ((0, 1), (1, 0)))


def full(dims):
    return pl.BlockSpec(dims, lambda *_: (0,) * len(dims))


def column(dims, at):
    return pl.BlockSpec(dims, lambda step, heads: (0, heads[at]))


def body(tokens, occupancy, counts, queries, saved_lse, grad_out, attn_out, w_key, w_value):
    tokens, grad, out, lse = tokens[0], grad_out[0], attn_out[0], saved_lse[0]
    shard, width = tokens.shape
    latents, rows = queries.shape[0], grad.shape[0]
    chips, groups, windows = lax.axis_size("x"), lax.axis_size("z"), lax.axis_size("y")
    heads = lse.shape[1]
    core = lax.axis_index("c").astype(jnp.int32)
    head = 2 * lax.axis_index("x").astype(jnp.int32) + core
    head_pair = jnp.stack([head, head + 1 - 2 * core])
    core = core.reshape(1)
    tokens, head_pair, core = lax.optimization_barrier((tokens, head_pair, core))
    sent = pl.pallas_call(
        pack_kernel,
        out_shape=shape((chips, shard + 2 * rows, width)),
        in_specs=[pl.BlockSpec(memory_space=pltpu.HBM)] * 6,
        out_specs=VMEM,
        scratch_shapes=[pltpu.SMEM(counts.shape, counts.dtype)]
        + [pltpu.VMEM(ref.shape, ref.dtype) for ref in (tokens, occupancy, grad, out, lse)]
        + [pltpu.SemaphoreType.DMA((6,))],
        compiler_params=params(60),
    )(counts, tokens, occupancy, grad, out, lse)
    got = swap(sent, "x")
    other = sibling(got)
    grads = pl.pallas_call(
        turn_kernel,
        out_shape=shape((2 * groups, rows * chips, width)),
        in_specs=[VMEM],
        out_specs=VMEM,
        compiler_params=params(8),
    )(got)
    grads = swap(grads, ("z", "c"))

    each, half = width // groups, rows * heads // 2
    back = (chips, shard, width)
    part = (groups, each + half, width)
    keep, give, parts = pl.pallas_call(
        main_kernel,
        out_shape=(shape(back), shape(back), shape(part)),
        grid_spec=pltpu.PrefetchScalarGridSpec(
            num_scalar_prefetch=1,
            grid=(1,),
            in_specs=[
                full(got.shape),
                full(other.shape),
                full(grads.shape),
                column((latents, HEAD), 0),
                column((width, HEAD), 0),
                column((width, HEAD), 0),
            ],
            out_specs=[full(back), full(back), full(part)],
            scratch_shapes=[pltpu.VMEM((HEAD, latents), F32), pltpu.VMEM((width, width), F32)],
        ),
        compiler_params=params(40),
    )(head_pair, got, other, grads, queries, w_key, w_value)

    theirs, parts = lax.optimization_barrier((sibling(give), swap(parts, "z")))
    parts = pl.pallas_call(
        spread_kernel,
        out_shape=shape((windows, each + half, width)),
        in_specs=[VMEM],
        out_specs=VMEM,
        compiler_params=params(8),
    )(parts)
    parts = swap(parts, "y")
    weights, query_part = pl.pallas_call(
        total_kernel,
        out_shape=(shape((groups, each, width)), shape((2 * half, HEAD), F32)),
        in_specs=[VMEM],
        out_specs=(VMEM, VMEM),
        compiler_params=params(8),
    )(parts)
    weights = swap(weights, "z").reshape(width, width)
    last = (chips, shard + width + 2 * rows, width)
    sent = pl.pallas_call(
        gather_kernel,
        out_shape=shape(last),
        grid_spec=pltpu.PrefetchScalarGridSpec(
            num_scalar_prefetch=1,
            grid=(1,),
            in_specs=[full(back), full(back), full(weights.shape), full(query_part.shape)]
            + [column((width, HEAD), at) for at in (0, 0, 1, 1)],
            out_specs=full(last),
        ),
        compiler_params=params(20),
    )(head_pair, keep, theirs, weights, query_part, w_key, w_value, w_key, w_value)
    got = swap(sent, "x")
    other = sibling(got)
    grad_tokens = pl.pallas_call(
        tokens_kernel,
        out_shape=shape((shard, width)),
        in_specs=[SMEM] + [VMEM] * 3,
        out_specs=VMEM,
        compiler_params=params(16),
        cost_estimate=pl.CostEstimate(flops=2000000, bytes_accessed=1000000, transcendentals=256),
    )(counts, got, tokens, occupancy)
    query_rows, key_total, value_total = pl.pallas_call(
        finish_kernel,
        out_shape=(
            shape((rows, heads * HEAD), F32),
            shape((width, heads * HEAD), F32),
            shape((width, heads * HEAD), F32),
        ),
        in_specs=[SMEM] + [VMEM] * 2,
        out_specs=(VMEM,) * 3,
        compiler_params=params(16),
    )(core, got, other)
    return grad_tokens[None], query_rows, key_total, value_total


def solution(mesh):
    seq, dp = mesh.shape["seq"], mesh.shape["dp"]
    split = Mesh(mesh.devices.reshape(seq // 8, 4, 2, dp), ("z", "x", "c", "y"))
    both = ("z", "x", "c")
    rows = P("y", both, None)
    return jax.shard_map(
        body,
        mesh=split,
        in_specs=(rows, P("y", both), P("y", both), P(), rows, rows, rows, P(), P()),
        out_specs=(rows, P(both, None), P(), P()),
        check_vma=False,
    )
```

```python
import math

import jax
import jax.numpy as jnp
from jax import lax
from jax.experimental import pallas as pl
from jax.experimental.pallas import tpu as pltpu
from jax.sharding import Mesh
from jax.sharding import PartitionSpec as P

HEAD = 128
ROWS = 8
EPS = 1e-05
LOG2E = math.log2(math.e)
F32, BF16 = jnp.float32, jnp.bfloat16
VMEM = pl.BlockSpec(memory_space=pltpu.VMEM)
SMEM = pl.BlockSpec(memory_space=pltpu.SMEM)


def params(mib):
    return pltpu.CompilerParams(vmem_limit_bytes=mib * 1024 * 1024)


def mm(left, right, left_dim, right_dim):
    return lax.dot_general(
        left, right, (((left_dim,), (right_dim,)), ((), ())), preferred_element_type=F32
    )


def layer_norm(tokens):
    center = tokens - jnp.mean(tokens, axis=-1, keepdims=True)
    inverse = lax.rsqrt(jnp.mean(center * center, axis=-1, keepdims=True) + EPS)
    return center * inverse, inverse


def live_rows(occupancy, count, width):
    shard = occupancy.shape[1]
    place = lax.broadcasted_iota(jnp.int32, (1, shard), 1)
    live = jnp.where(place < count, occupancy, 0).astype(F32)
    return jnp.broadcast_to(live, (width, shard)).T


def three_parts(column):
    parts = []
    for _ in range(3):
        part = column.astype(BF16).astype(F32)
        parts.append(part)
        column = column - part
    return parts


def pack_kernel(*refs):
    sources, sent, (counts, tokens, occupancy, grad, out, lse), done = (
        refs[:6],
        refs[6],
        refs[7:13],
        refs[13],
    )
    copies = [
        pltpu.make_async_copy(source, target, done.at[at])
        for at, (source, target) in enumerate(zip(sources, refs[7:13]))
    ]
    for copy in copies:
        copy.start()
    for copy in copies:
        copy.wait()
    chips, (shard, width) = sent.shape[0], tokens.shape
    live = live_rows(occupancy[...], counts[0, 0], width)
    masked = jnp.where(live > 0.0, tokens[...].astype(F32), 0.0).astype(BF16)
    rows = grad.shape[0]
    lane = lax.broadcasted_iota(jnp.int32, (rows, HEAD), 1)
    for chip in range(chips):
        sent[chip, :shard, :] = masked
        extras, grads = [], []
        for head in (2 * chip, 2 * chip + 1):
            cols = slice(head * HEAD, (head + 1) * HEAD)
            grad_f32 = grad[:, cols].astype(F32)
            delta = jnp.sum(grad_f32 * out[:, cols].astype(F32), axis=1, keepdims=True)
            extra = jnp.zeros((rows, HEAD), F32)
            for at, part in enumerate(three_parts(lse[:, head : head + 1]) + three_parts(delta)):
                extra = jnp.where(lane == at, part, extra)
            extras.append(extra)
            grads.append(grad_f32)
        both = jnp.concatenate(
            [jnp.concatenate(grads, axis=1), jnp.concatenate(extras, axis=1)], axis=0
        )
        sent[chip, shard:, :] = both.astype(BF16)


def turn_kernel(got, sent):
    chips, width = got.shape[0], got.shape[2]
    shard = got.shape[1] - sent.shape[1] // chips * 2
    pieces = [got[chip, shard:, :].astype(F32) for chip in range(chips)]
    rows = sent.shape[1] // chips
    grads = jnp.concatenate([piece[:rows] for piece in pieces], axis=0)
    extras = jnp.concatenate([piece[rows:] for piece in pieces], axis=0)
    for core in range(2):
        cols = slice(core * HEAD, (core + 1) * HEAD)
        both = jnp.concatenate([grads[:, cols], extras[:, cols]], axis=1).astype(BF16)
        for group in range(sent.shape[0] // 2):
            sent[2 * group + core] = both


def latent_order(got, chips):
    rows = got.shape[1] // chips
    blocks = [got[at].astype(F32) for at in range(got.shape[0])]
    return jnp.concatenate(
        [
            blocks[2 * group + core][chip * rows : (chip + 1) * rows]
            for group in range(got.shape[0] // 2)
            for chip in range(chips)
            for core in range(2)
        ],
        axis=0,
    )


def main_kernel(
    head, mine, other, got, query, w_key, w_value, keep, give, parts, query_sum, weight_sum
):
    del head
    chips, shard = keep.shape[0], keep.shape[1]
    scale = 1.0 / math.sqrt(HEAD)
    rows = latent_order(got, chips)
    grad = rows[:, :HEAD].astype(BF16)
    extra = rows[:, HEAD:].T
    lse = (extra[0:1] + extra[1:2] + extra[2:3]) * LOG2E
    delta = extra[3:4] + extra[4:5] + extra[5:6]
    queries = query[...]
    weights = jnp.concatenate([w_key[...], w_value[...]], axis=1)
    for block in range(2 * chips):
        source, target = (mine, keep) if block < chips else (other, give)
        chip = block % chips
        normal = layer_norm(source[chip, :shard, :].astype(F32))[0].astype(BF16)
        both = jnp.dot(normal, weights, preferred_element_type=F32).astype(BF16)
        keys, values = both[:, :HEAD], both[:, HEAD:]
        probs = jnp.exp2(mm(keys, queries, 1, 1) * (scale * LOG2E) - lse)
        grad_values = jnp.dot(probs.astype(BF16), grad, preferred_element_type=F32)
        grad_probs = mm(values, grad, 1, 1)
        grad_scores = (scale * probs * (grad_probs - delta)).astype(BF16)
        grad_keys = jnp.dot(grad_scores, queries, preferred_element_type=F32)
        grad_both = jnp.concatenate([grad_keys, grad_values], axis=1).astype(BF16)
        target[chip] = grad_both
        query_part = mm(keys, grad_scores, 0, 0)
        weight_part = mm(normal, grad_both, 0, 0)
        if block == 0:
            query_sum[...] = query_part
            weight_sum[...] = weight_part
        else:
            query_sum[...] += query_part
            weight_sum[...] += weight_part
    turned = query_sum[...].T
    totals = weight_sum[...]
    halves = parts.shape[0] // 2
    for at in range(parts.shape[0]):
        start = at % halves * ROWS
        cols = slice(at // halves * HEAD, (at // halves + 1) * HEAD)
        piece = [totals[start : start + ROWS, cols], turned[at * ROWS : (at + 1) * ROWS]]
        parts[at] = jnp.concatenate(piece, axis=1).astype(BF16)


def add_up(got):
    total = got[0].astype(F32)
    for at in range(1, got.shape[0]):
        total = total + got[at].astype(F32)
    return total


def spread_kernel(got, sent):
    total = add_up(got).astype(BF16)
    for at in range(sent.shape[0]):
        sent[at] = total


def gather_kernel(
    places, keep, theirs, got, my_key, my_value, their_key, their_value, sent
):
    chips, shard = keep.shape[0], keep.shape[1]
    halves = got.shape[0] // 2
    depth = halves * ROWS
    mine = jnp.concatenate([my_key[...], my_value[...]], axis=1)
    other = jnp.concatenate([their_key[...], their_value[...]], axis=1)
    pieces = [got[at].astype(F32)[:, :HEAD] for at in range(2 * halves)]
    weights = jnp.concatenate(
        [jnp.concatenate(pieces[:halves], axis=0), jnp.concatenate(pieces[halves:], axis=0)], axis=1
    ).astype(BF16)
    for chip in range(chips):
        grad_normal = mm(keep[chip], mine, 1, 1) + mm(theirs[chip], other, 1, 1)
        sent[chip, :shard, :] = grad_normal.astype(BF16)
        sent[chip, shard : shard + depth, :] = weights
        first = places[2] * 2 * chips + 2 * chip
        rows = [got[first + core].astype(F32) for core in range(2)]
        sent[chip, shard + depth :, :] = jnp.concatenate(rows, axis=0).astype(BF16)


def tokens_kernel(counts, got, tokens, occupancy, grad_tokens):
    chips, (shard, width) = got.shape[0], tokens.shape
    normal, inverse = layer_norm(tokens[...].astype(F32))
    grad_normal = got[0, :shard, :].astype(F32)
    for chip in range(1, chips):
        grad_normal += got[chip, :shard, :].astype(F32)
    live = live_rows(occupancy[...], counts[0, 0], width)
    grad_normal = jnp.where(live > 0.0, grad_normal, 0.0)
    grad_input = inverse * (
        grad_normal
        - jnp.mean(grad_normal, axis=-1, keepdims=True)
        - normal * jnp.mean(grad_normal * normal, axis=-1, keepdims=True)
    )
    grad_tokens[...] = grad_input.astype(BF16)


def finish_kernel(core, got, other, query_rows, key_total, value_total):
    chips, depth, rows = got.shape[0], key_total.shape[0], query_rows.shape[0]
    shard = got.shape[1] - depth - 2 * rows

    def write(low, high):
        for chip in range(chips):
            for at, source in ((2 * chip, low), (2 * chip + 1, high)):
                cols = slice(at * HEAD, (at + 1) * HEAD)
                both = source[chip, shard : shard + depth, :].astype(F32)
                key_total[:, cols] = both[:, :HEAD]
                value_total[:, cols] = both[:, HEAD:]
                piece = source[chip, shard + depth :, :].astype(F32)
                both_rows = piece[:, HEAD:]
                query_rows[:, cols] = jnp.where(core[0] == 0, both_rows[:rows], both_rows[rows:])

    @pl.when(core[0] == 0)
    def _():
        write(got, other)

    @pl.when(core[0] != 0)
    def _():
        write(other, got)


def swap(array, axis):
    return lax.all_to_all(array, axis, 0, 0, tiled=True)


def shape(dims, dtype=BF16):
    return jax.ShapeDtypeStruct(dims, dtype)


def sibling(array):
    return lax.ppermute(array, "c", ((0, 1), (1, 0)))


def full(dims):
    return pl.BlockSpec(dims, lambda *_: (0,) * len(dims))


def column(dims, at):
    return pl.BlockSpec(dims, lambda step, heads: (0, heads[at]))


def body(tokens, occupancy, counts, queries, saved_lse, grad_out, attn_out, w_key, w_value):
    tokens, grad, out, lse = tokens[0], grad_out[0], attn_out[0], saved_lse[0]
    shard, width = tokens.shape
    latents, rows = queries.shape[0], grad.shape[0]
    chips, groups, windows = lax.axis_size("x"), lax.axis_size("z"), lax.axis_size("y")
    heads = lse.shape[1]
    core = lax.axis_index("c").astype(jnp.int32)
    head = 2 * lax.axis_index("x").astype(jnp.int32) + core
    head_pair = jnp.stack([head, head + 1 - 2 * core, lax.axis_index("z").astype(jnp.int32)])
    core = core.reshape(1)
    tokens, head_pair, core = lax.optimization_barrier((tokens, head_pair, core))
    sent = pl.pallas_call(
        pack_kernel,
        out_shape=shape((chips, shard + 2 * rows, width)),
        in_specs=[pl.BlockSpec(memory_space=pltpu.HBM)] * 6,
        out_specs=VMEM,
        scratch_shapes=[pltpu.SMEM(counts.shape, counts.dtype)]
        + [pltpu.VMEM(ref.shape, ref.dtype) for ref in (tokens, occupancy, grad, out, lse)]
        + [pltpu.SemaphoreType.DMA((6,))],
        compiler_params=params(60),
    )(counts, tokens, occupancy, grad, out, lse)
    got = swap(sent, "x")
    other = sibling(got)
    grads = pl.pallas_call(
        turn_kernel,
        out_shape=shape((2 * groups, rows * chips, width)),
        in_specs=[VMEM],
        out_specs=VMEM,
        compiler_params=params(8),
    )(got)
    grads = swap(grads, ("z", "c"))

    back = (chips, shard, width)
    part = (groups * windows, ROWS, width)
    keep, give, parts = pl.pallas_call(
        main_kernel,
        out_shape=(shape(back), shape(back), shape(part)),
        grid_spec=pltpu.PrefetchScalarGridSpec(
            num_scalar_prefetch=1,
            grid=(1,),
            in_specs=[
                full(got.shape),
                full(other.shape),
                full(grads.shape),
                column((latents, HEAD), 0),
                column((width, HEAD), 0),
                column((width, HEAD), 0),
            ],
            out_specs=[full(back), full(back), full(part)],
            scratch_shapes=[pltpu.VMEM((HEAD, latents), F32), pltpu.VMEM((width, width), F32)],
        ),
        compiler_params=params(40),
    )(head_pair, got, other, grads, queries, w_key, w_value)

    theirs, parts = lax.optimization_barrier((sibling(give), swap(parts, ("z", "y"))))
    parts = pl.pallas_call(
        spread_kernel,
        out_shape=shape(part),
        in_specs=[VMEM],
        out_specs=VMEM,
        compiler_params=params(8),
    )(parts)
    parts = swap(parts, ("z", "y"))
    last = (chips, shard + width + 2 * rows, width)
    sent = pl.pallas_call(
        gather_kernel,
        out_shape=shape(last),
        grid_spec=pltpu.PrefetchScalarGridSpec(
            num_scalar_prefetch=1,
            grid=(1,),
            in_specs=[full(back), full(back), full(part)]
            + [column((width, HEAD), at) for at in (0, 0, 1, 1)],
            out_specs=full(last),
        ),
        compiler_params=params(20),
    )(head_pair, keep, theirs, parts, w_key, w_value, w_key, w_value)
    got = swap(sent, "x")
    other = sibling(got)
    grad_tokens = pl.pallas_call(
        tokens_kernel,
        out_shape=shape((shard, width)),
        in_specs=[SMEM] + [VMEM] * 3,
        out_specs=VMEM,
        compiler_params=params(16),
        cost_estimate=pl.CostEstimate(flops=2000000, bytes_accessed=1000000, transcendentals=256),
    )(counts, got, tokens, occupancy)
    query_rows, key_total, value_total = pl.pallas_call(
        finish_kernel,
        out_shape=(
            shape((rows, heads * HEAD), F32),
            shape((width, heads * HEAD), F32),
            shape((width, heads * HEAD), F32),
        ),
        in_specs=[SMEM] + [VMEM] * 2,
        out_specs=(VMEM,) * 3,
        compiler_params=params(16),
    )(core, got, other)
    return grad_tokens[None], query_rows, key_total, value_total


def solution(mesh):
    seq, dp = mesh.shape["seq"], mesh.shape["dp"]
    split = Mesh(mesh.devices.reshape(seq // 8, 4, 2, dp), ("z", "x", "c", "y"))
    both = ("z", "x", "c")
    rows = P("y", both, None)
    return jax.shard_map(
        body,
        mesh=split,
        in_specs=(rows, P("y", both), P("y", both), P(), rows, rows, rows, P(), P()),
        out_specs=(rows, P(both, None), P(), P()),
        check_vma=False,
    )
```

```python
import math

import jax
import jax.numpy as jnp
from jax import lax
from jax.experimental import pallas as pl
from jax.experimental.pallas import tpu as pltpu
from jax.sharding import Mesh
from jax.sharding import PartitionSpec as P

HEAD = 128
ROWS = 8
BLOCK = 512
EPS = 1e-05
LOG2E = math.log2(math.e)
F32, BF16 = jnp.float32, jnp.bfloat16
VMEM = pl.BlockSpec(memory_space=pltpu.VMEM)
SMEM = pl.BlockSpec(memory_space=pltpu.SMEM)


def params(mib):
    return pltpu.CompilerParams(vmem_limit_bytes=mib * 1024 * 1024)


def mm(left, right, left_dim, right_dim):
    return lax.dot_general(
        left, right, (((left_dim,), (right_dim,)), ((), ())), preferred_element_type=F32
    )


def layer_norm(tokens):
    center = tokens - jnp.mean(tokens, axis=-1, keepdims=True)
    inverse = lax.rsqrt(jnp.mean(center * center, axis=-1, keepdims=True) + EPS)
    return center * inverse, inverse


def live_rows(occupancy, count, width):
    shard = occupancy.shape[1]
    place = lax.broadcasted_iota(jnp.int32, (1, shard), 1)
    live = jnp.where(place < count, occupancy, 0).astype(F32)
    return jnp.broadcast_to(live, (width, shard)).T


def three_parts(column):
    parts = []
    for _ in range(3):
        part = column.astype(BF16).astype(F32)
        parts.append(part)
        column = column - part
    return parts


def pack_kernel(*refs):
    sources, sent, (counts, tokens, occupancy, grad, out, lse), done = (
        refs[:6],
        refs[6],
        refs[7:13],
        refs[13],
    )
    copies = [
        pltpu.make_async_copy(source, target, done.at[at])
        for at, (source, target) in enumerate(zip(sources, refs[7:13]))
    ]
    for copy in copies:
        copy.start()
    for copy in copies:
        copy.wait()
    chips, (shard, width) = sent.shape[0], tokens.shape
    live = live_rows(occupancy[...], counts[0, 0], width)
    masked = jnp.where(live > 0.0, tokens[...].astype(F32), 0.0).astype(BF16)
    rows = grad.shape[0]
    lane = lax.broadcasted_iota(jnp.int32, (rows, HEAD), 1)
    for chip in range(chips):
        sent[chip, :shard, :] = masked
        extras, grads = [], []
        for head in (2 * chip, 2 * chip + 1):
            cols = slice(head * HEAD, (head + 1) * HEAD)
            grad_f32 = grad[:, cols].astype(F32)
            delta = jnp.sum(grad_f32 * out[:, cols].astype(F32), axis=1, keepdims=True)
            extra = jnp.zeros((rows, HEAD), F32)
            for at, part in enumerate(three_parts(lse[:, head : head + 1]) + three_parts(delta)):
                extra = jnp.where(lane == at, part, extra)
            extras.append(extra)
            grads.append(grad_f32)
        both = jnp.concatenate(
            [jnp.concatenate(grads, axis=1), jnp.concatenate(extras, axis=1)], axis=0
        )
        sent[chip, shard:, :] = both.astype(BF16)


def turn_kernel(got, sent):
    chips, width = got.shape[0], got.shape[2]
    shard = got.shape[1] - sent.shape[1] // chips * 2
    pieces = [got[chip, shard:, :].astype(F32) for chip in range(chips)]
    rows = sent.shape[1] // chips
    grads = jnp.concatenate([piece[:rows] for piece in pieces], axis=0)
    extras = jnp.concatenate([piece[rows:] for piece in pieces], axis=0)
    for core in range(2):
        cols = slice(core * HEAD, (core + 1) * HEAD)
        both = jnp.concatenate([grads[:, cols], extras[:, cols]], axis=1).astype(BF16)
        for group in range(sent.shape[0] // 2):
            sent[2 * group + core] = both


def latent_order(got, chips):
    rows = got.shape[1] // chips
    blocks = [got[at].astype(F32) for at in range(got.shape[0])]
    return jnp.concatenate(
        [
            blocks[2 * group + core][chip * rows : (chip + 1) * rows]
            for group in range(got.shape[0] // 2)
            for chip in range(chips)
            for core in range(2)
        ],
        axis=0,
    )


def share_kernel(head, keep, give, w_key, w_value, kept, given):
    del head
    weights = jnp.concatenate([w_key[...], w_value[...]], axis=1)
    for chip in range(keep.shape[0]):
        kept[chip] = mm(keep[chip], weights, 1, 1)
        given[chip] = mm(give[chip], weights, 1, 1).astype(BF16)


def main_kernel(
    head, mine, other, got, query, w_key, w_value, keep, give, parts, query_sum, normals, grads
):
    del head
    chips, shard = keep.shape[0], keep.shape[1]
    scale = 1.0 / math.sqrt(HEAD)
    rows = latent_order(got, chips)
    grad = rows[:, :HEAD].astype(BF16)
    extra = rows[:, HEAD:].T
    lse = (extra[0:1] + extra[1:2] + extra[2:3]) * LOG2E
    delta = extra[3:4] + extra[4:5] + extra[5:6]
    queries = query[...]
    weights = jnp.concatenate([w_key[...], w_value[...]], axis=1)
    per = BLOCK // shard
    for block in range(2 * chips // per):
        first = block * per
        source, target = (mine, keep) if first < chips else (other, give)
        spots = [(first + at) % chips for at in range(per)]
        tokens = jnp.concatenate([source[spot, :shard, :] for spot in spots], axis=0)
        normal = layer_norm(tokens.astype(F32))[0].astype(BF16)
        both = jnp.dot(normal, weights, preferred_element_type=F32).astype(BF16)
        keys, values = both[:, :HEAD], both[:, HEAD:]
        probs = jnp.exp2(mm(keys, queries, 1, 1) * (scale * LOG2E) - lse)
        grad_values = jnp.dot(probs.astype(BF16), grad, preferred_element_type=F32)
        grad_probs = mm(values, grad, 1, 1)
        grad_scores = (scale * probs * (grad_probs - delta)).astype(BF16)
        grad_keys = jnp.dot(grad_scores, queries, preferred_element_type=F32)
        grad_both = jnp.concatenate([grad_keys, grad_values], axis=1).astype(BF16)
        for at, spot in enumerate(spots):
            target[spot] = grad_both[at * shard : (at + 1) * shard]
        query_part = mm(keys, grad_scores, 0, 0)
        if block == 0:
            query_sum[...] = query_part
        else:
            query_sum[...] += query_part
        normals[block * BLOCK : (block + 1) * BLOCK, :] = normal
        grads[block * BLOCK : (block + 1) * BLOCK, :] = grad_both
    turned = query_sum[...].T
    totals = mm(normals[...], grads[...], 0, 0)
    halves = parts.shape[0] // 2
    for at in range(parts.shape[0]):
        start = at % halves * ROWS
        cols = slice(at // halves * HEAD, (at // halves + 1) * HEAD)
        piece = [totals[start : start + ROWS, cols], turned[at * ROWS : (at + 1) * ROWS]]
        parts[at] = jnp.concatenate(piece, axis=1).astype(BF16)


def add_up(got):
    total = got[0].astype(F32)
    for at in range(1, got.shape[0]):
        total = total + got[at].astype(F32)
    return total


def spread_kernel(got, sent):
    total = add_up(got).astype(BF16)
    for at in range(sent.shape[0]):
        sent[at] = total


def gather_kernel(group, kept, theirs, got, sent):
    chips, shard = kept.shape[0], kept.shape[1]
    halves = got.shape[0] // 2
    depth = halves * ROWS
    pieces = [got[at].astype(F32)[:, :HEAD] for at in range(2 * halves)]
    weights = jnp.concatenate(
        [jnp.concatenate(pieces[:halves], axis=0), jnp.concatenate(pieces[halves:], axis=0)], axis=1
    ).astype(BF16)
    for chip in range(chips):
        sent[chip, :shard, :] = (kept[chip] + theirs[chip].astype(F32)).astype(BF16)
        sent[chip, shard : shard + depth, :] = weights
        first = group[0] * 2 * chips + 2 * chip
        rows = [got[first + core].astype(F32) for core in range(2)]
        sent[chip, shard + depth :, :] = jnp.concatenate(rows, axis=0).astype(BF16)


def tokens_kernel(counts, got, tokens, occupancy, grad_tokens):
    chips, (shard, width) = got.shape[0], tokens.shape
    normal, inverse = layer_norm(tokens[...].astype(F32))
    grad_normal = got[0, :shard, :].astype(F32)
    for chip in range(1, chips):
        grad_normal += got[chip, :shard, :].astype(F32)
    live = live_rows(occupancy[...], counts[0, 0], width)
    grad_normal = jnp.where(live > 0.0, grad_normal, 0.0)
    grad_input = inverse * (
        grad_normal
        - jnp.mean(grad_normal, axis=-1, keepdims=True)
        - normal * jnp.mean(grad_normal * normal, axis=-1, keepdims=True)
    )
    grad_tokens[...] = grad_input.astype(BF16)


def finish_kernel(core, got, other, query_rows, key_total, value_total):
    chips, depth, rows = got.shape[0], key_total.shape[0], query_rows.shape[0]
    shard = got.shape[1] - depth - 2 * rows

    def write(low, high):
        for chip in range(chips):
            for at, source in ((2 * chip, low), (2 * chip + 1, high)):
                cols = slice(at * HEAD, (at + 1) * HEAD)
                both = source[chip, shard : shard + depth, :].astype(F32)
                key_total[:, cols] = both[:, :HEAD]
                value_total[:, cols] = both[:, HEAD:]
                piece = source[chip, shard + depth :, :].astype(F32)
                both_rows = piece[:, HEAD:]
                query_rows[:, cols] = jnp.where(core[0] == 0, both_rows[:rows], both_rows[rows:])

    @pl.when(core[0] == 0)
    def _():
        write(got, other)

    @pl.when(core[0] != 0)
    def _():
        write(other, got)


def swap(array, axis):
    return lax.all_to_all(array, axis, 0, 0, tiled=True)


def shape(dims, dtype=BF16):
    return jax.ShapeDtypeStruct(dims, dtype)


def sibling(array):
    return lax.ppermute(array, "c", ((0, 1), (1, 0)))


def full(dims):
    return pl.BlockSpec(dims, lambda *_: (0,) * len(dims))


def column(dims, at):
    return pl.BlockSpec(dims, lambda step, heads: (0, heads[at]))


def body(tokens, occupancy, counts, queries, saved_lse, grad_out, attn_out, w_key, w_value):
    tokens, grad, out, lse = tokens[0], grad_out[0], attn_out[0], saved_lse[0]
    shard, width = tokens.shape
    latents, rows = queries.shape[0], grad.shape[0]
    chips, groups, windows = lax.axis_size("x"), lax.axis_size("z"), lax.axis_size("y")
    heads = lse.shape[1]
    core = lax.axis_index("c").astype(jnp.int32)
    head = (2 * lax.axis_index("x").astype(jnp.int32) + core).reshape(1)
    core, group = core.reshape(1), lax.axis_index("z").astype(jnp.int32).reshape(1)
    tokens, head, core, group = lax.optimization_barrier((tokens, head, core, group))
    sent = pl.pallas_call(
        pack_kernel,
        out_shape=shape((chips, shard + 2 * rows, width)),
        in_specs=[pl.BlockSpec(memory_space=pltpu.HBM)] * 6,
        out_specs=VMEM,
        scratch_shapes=[pltpu.SMEM(counts.shape, counts.dtype)]
        + [pltpu.VMEM(ref.shape, ref.dtype) for ref in (tokens, occupancy, grad, out, lse)]
        + [pltpu.SemaphoreType.DMA((6,))],
        compiler_params=params(60),
    )(counts, tokens, occupancy, grad, out, lse)
    got = swap(sent, "x")
    other = sibling(got)
    grads = pl.pallas_call(
        turn_kernel,
        out_shape=shape((2 * groups, rows * chips, width)),
        in_specs=[VMEM],
        out_specs=VMEM,
        compiler_params=params(8),
    )(got)
    grads = swap(grads, ("z", "c"))

    back = (chips, shard, width)
    part = (groups * windows, ROWS, width)
    keep, give, parts = pl.pallas_call(
        main_kernel,
        out_shape=(shape(back), shape(back), shape(part)),
        grid_spec=pltpu.PrefetchScalarGridSpec(
            num_scalar_prefetch=1,
            grid=(1,),
            in_specs=[
                full(got.shape),
                full(other.shape),
                full(grads.shape),
                column((latents, HEAD), 0),
                column((width, HEAD), 0),
                column((width, HEAD), 0),
            ],
            out_specs=[full(back), full(back), full(part)],
            scratch_shapes=[pltpu.VMEM((HEAD, latents), F32)]
            + [pltpu.VMEM((2 * chips * shard, width), BF16)] * 2,
        ),
        compiler_params=params(40),
    )(head, got, other, grads, queries, w_key, w_value)

    kept, given = pl.pallas_call(
        share_kernel,
        out_shape=(shape(back, F32), shape(back)),
        grid_spec=pltpu.PrefetchScalarGridSpec(
            num_scalar_prefetch=1,
            grid=(1,),
            in_specs=[full(back)] * 2 + [column((width, HEAD), 0)] * 2,
            out_specs=[full(back)] * 2,
        ),
        compiler_params=params(20),
        cost_estimate=pl.CostEstimate(flops=270000000, bytes_accessed=3000000, transcendentals=0),
    )(head, keep, give, w_key, w_value)
    theirs = sibling(given)
    parts = swap(parts, ("z", "y"))
    parts = pl.pallas_call(
        spread_kernel,
        out_shape=shape(part),
        in_specs=[VMEM],
        out_specs=VMEM,
        compiler_params=params(8),
    )(parts)
    parts = swap(parts, ("z", "y"))
    last = (chips, shard + width + 2 * rows, width)
    sent = pl.pallas_call(
        gather_kernel,
        out_shape=shape(last),
        in_specs=[SMEM] + [VMEM] * 3,
        out_specs=VMEM,
        compiler_params=params(16),
    )(group, kept, theirs, parts)
    got = swap(sent, "x")
    other = sibling(got)
    grad_tokens = pl.pallas_call(
        tokens_kernel,
        out_shape=shape((shard, width)),
        in_specs=[SMEM] + [VMEM] * 3,
        out_specs=VMEM,
        compiler_params=params(16),
        cost_estimate=pl.CostEstimate(flops=2000000, bytes_accessed=1000000, transcendentals=256),
    )(counts, got, tokens, occupancy)
    query_rows, key_total, value_total = pl.pallas_call(
        finish_kernel,
        out_shape=(
            shape((rows, heads * HEAD), F32),
            shape((width, heads * HEAD), F32),
            shape((width, heads * HEAD), F32),
        ),
        in_specs=[SMEM] + [VMEM] * 2,
        out_specs=(VMEM,) * 3,
        compiler_params=params(16),
    )(core, got, other)
    return grad_tokens[None], query_rows, key_total, value_total


def solution(mesh):
    seq, dp = mesh.shape["seq"], mesh.shape["dp"]
    split = Mesh(mesh.devices.reshape(seq // 8, 4, 2, dp), ("z", "x", "c", "y"))
    both = ("z", "x", "c")
    rows = P("y", both, None)
    return jax.shard_map(
        body,
        mesh=split,
        in_specs=(rows, P("y", both), P("y", both), P(), rows, rows, rows, P(), P()),
        out_specs=(rows, P(both, None), P(), P()),
        check_vma=False,
    )
```

```python
import math

import jax
import jax.numpy as jnp
from jax import lax
from jax.experimental import pallas as pl
from jax.experimental.pallas import tpu as pltpu
from jax.sharding import Mesh
from jax.sharding import PartitionSpec as P

HEAD = 128
ROWS = 8
BLOCK = 512
EPS = 1e-05
LOG2E = math.log2(math.e)
F32, BF16 = jnp.float32, jnp.bfloat16
VMEM = pl.BlockSpec(memory_space=pltpu.VMEM)
HBM = pl.BlockSpec(memory_space=pltpu.HBM)
SMEM = pl.BlockSpec(memory_space=pltpu.SMEM)


def params(mib):
    return pltpu.CompilerParams(vmem_limit_bytes=mib * 1024 * 1024)


def mm(left, right, left_dim, right_dim):
    return lax.dot_general(
        left, right, (((left_dim,), (right_dim,)), ((), ())), preferred_element_type=F32
    )


def layer_norm(tokens):
    center = tokens - jnp.mean(tokens, axis=-1, keepdims=True)
    inverse = lax.rsqrt(jnp.mean(center * center, axis=-1, keepdims=True) + EPS)
    return center * inverse, inverse


def live_rows(occupancy, count, width):
    shard = occupancy.shape[1]
    place = lax.broadcasted_iota(jnp.int32, (1, shard), 1)
    live = jnp.where(place < count, occupancy, 0).astype(F32)
    return jnp.broadcast_to(live, (width, shard)).T


def three_parts(column):
    parts = []
    for _ in range(3):
        part = column.astype(BF16).astype(F32)
        parts.append(part)
        column = column - part
    return parts


def pack_kernel(*refs):
    sources, sent, (counts, tokens, occupancy, grad, out, lse), done = (
        refs[:6],
        refs[6],
        refs[7:13],
        refs[13],
    )
    copies = [
        pltpu.make_async_copy(source, target, done.at[at])
        for at, (source, target) in enumerate(zip(sources, refs[7:13]))
    ]
    for copy in copies:
        copy.start()
    for copy in copies:
        copy.wait()
    chips, (shard, width) = sent.shape[0], tokens.shape
    live = live_rows(occupancy[...], counts[0, 0], width)
    masked = jnp.where(live > 0.0, tokens[...].astype(F32), 0.0).astype(BF16)
    rows = grad.shape[0]
    lane = lax.broadcasted_iota(jnp.int32, (rows, HEAD), 1)
    for chip in range(chips):
        sent[chip, :shard, :] = masked
        extras, grads = [], []
        for head in (2 * chip, 2 * chip + 1):
            cols = slice(head * HEAD, (head + 1) * HEAD)
            grad_f32 = grad[:, cols].astype(F32)
            delta = jnp.sum(grad_f32 * out[:, cols].astype(F32), axis=1, keepdims=True)
            extra = jnp.zeros((rows, HEAD), F32)
            for at, part in enumerate(three_parts(lse[:, head : head + 1]) + three_parts(delta)):
                extra = jnp.where(lane == at, part, extra)
            extras.append(extra)
            grads.append(grad_f32)
        both = jnp.concatenate(
            [jnp.concatenate(grads, axis=1), jnp.concatenate(extras, axis=1)], axis=0
        )
        sent[chip, shard:, :] = both.astype(BF16)


def turn_kernel(got, sent):
    chips, width = got.shape[0], got.shape[2]
    shard = got.shape[1] - sent.shape[1] // chips * 2
    pieces = [got[chip, shard:, :].astype(F32) for chip in range(chips)]
    rows = sent.shape[1] // chips
    grads = jnp.concatenate([piece[:rows] for piece in pieces], axis=0)
    extras = jnp.concatenate([piece[rows:] for piece in pieces], axis=0)
    for core in range(2):
        cols = slice(core * HEAD, (core + 1) * HEAD)
        both = jnp.concatenate([grads[:, cols], extras[:, cols]], axis=1).astype(BF16)
        for group in range(sent.shape[0] // 2):
            sent[2 * group + core] = both


def latent_order(got, chips):
    rows = got.shape[1] // chips
    blocks = [got[at].astype(F32) for at in range(got.shape[0])]
    return jnp.concatenate(
        [
            blocks[2 * group + core][chip * rows : (chip + 1) * rows]
            for group in range(got.shape[0] // 2)
            for chip in range(chips)
            for core in range(2)
        ],
        axis=0,
    )


def share_kernel(head, keep, give, w_key, w_value, kept, given):
    del head
    weights = jnp.concatenate([w_key[...], w_value[...]], axis=1)
    shard = kept.shape[1]
    for chip in range(kept.shape[0]):
        rows = slice(chip * shard, (chip + 1) * shard)
        kept[chip] = mm(keep[rows, :], weights, 1, 1)
        given[chip] = mm(give[rows, :], weights, 1, 1).astype(BF16)


def attend(source, grad, lse, delta, queries, weights, target, query_sum, normals, grads, done):
    chips = source.shape[0]
    shard = target.shape[0] // chips
    scale = 1.0 / math.sqrt(HEAD)
    per = BLOCK // shard
    copies = []
    for block in range(chips // per):
        first = block * per
        rows = pl.ds(block * BLOCK, BLOCK)
        tokens = jnp.concatenate([source[first + at, :shard, :] for at in range(per)], axis=0)
        normal = layer_norm(tokens.astype(F32))[0].astype(BF16)
        both = jnp.dot(normal, weights, preferred_element_type=F32).astype(BF16)
        keys, values = both[:, :HEAD], both[:, HEAD:]
        probs = jnp.exp2(mm(keys, queries, 1, 1) * (scale * LOG2E) - lse)
        grad_values = jnp.dot(probs.astype(BF16), grad, preferred_element_type=F32)
        grad_probs = mm(values, grad, 1, 1)
        grad_scores = (scale * probs * (grad_probs - delta)).astype(BF16)
        grad_keys = jnp.dot(grad_scores, queries, preferred_element_type=F32)
        grad_both = jnp.concatenate([grad_keys, grad_values], axis=1).astype(BF16)
        query_sum[...] += mm(keys, grad_scores, 0, 0)
        normals[rows, :] = normal
        grads[rows, :] = grad_both
        copy = pltpu.make_async_copy(grads.at[rows], target.at[rows], done.at[block])
        copy.start()
        copies.append(copy)
    total = mm(normals[...], grads[...], 0, 0)
    for copy in copies:
        copy.wait()
    return total


def first_kernel(
    head, mine, got, query, w_key, w_value, keep, grad_rows, lines, query_sum, weight_sum, *scratch
):
    del head
    rows = latent_order(got, got.shape[1] // ROWS)
    grad = rows[:, :HEAD].astype(BF16)
    extra = rows[:, HEAD:].T
    lse = (extra[0:1] + extra[1:2] + extra[2:3]) * LOG2E
    delta = extra[3:4] + extra[4:5] + extra[5:6]
    grad_rows[...] = grad
    lines[...] = jnp.concatenate([lse, delta, jnp.zeros((ROWS - 2, rows.shape[0]), F32)], axis=0)
    weights = jnp.concatenate([w_key[...], w_value[...]], axis=1)
    query_sum[...] = jnp.zeros_like(query_sum)
    weight_sum[...] = attend(
        mine, grad, lse, delta, query[...], weights, keep, query_sum, *scratch
    )


def second_kernel(
    head,
    other,
    grad_rows,
    lines,
    query_sum,
    weight_sum,
    query,
    w_key,
    w_value,
    give,
    parts,
    total,
    *scratch,
):
    del head
    weights = jnp.concatenate([w_key[...], w_value[...]], axis=1)
    total[...] = query_sum[...]
    totals = weight_sum[...] + attend(
        other,
        grad_rows[...],
        lines[0:1, :],
        lines[1:2, :],
        query[...],
        weights,
        give,
        total,
        *scratch,
    )
    turned = total[...].T
    halves = parts.shape[0] // 2
    for at in range(parts.shape[0]):
        start = at % halves * ROWS
        cols = slice(at // halves * HEAD, (at // halves + 1) * HEAD)
        piece = [totals[start : start + ROWS, cols], turned[at * ROWS : (at + 1) * ROWS]]
        parts[at] = jnp.concatenate(piece, axis=1).astype(BF16)


def add_up(got):
    total = got[0].astype(F32)
    for at in range(1, got.shape[0]):
        total = total + got[at].astype(F32)
    return total


def spread_kernel(got, sent):
    total = add_up(got).astype(BF16)
    for at in range(sent.shape[0]):
        sent[at] = total


def gather_kernel(group, kept, theirs, got, sent):
    chips, shard = kept.shape[0], kept.shape[1]
    halves = got.shape[0] // 2
    depth = halves * ROWS
    pieces = [got[at].astype(F32)[:, :HEAD] for at in range(2 * halves)]
    weights = jnp.concatenate(
        [jnp.concatenate(pieces[:halves], axis=0), jnp.concatenate(pieces[halves:], axis=0)], axis=1
    ).astype(BF16)
    for chip in range(chips):
        sent[chip, :shard, :] = (kept[chip] + theirs[chip].astype(F32)).astype(BF16)
        sent[chip, shard : shard + depth, :] = weights
        first = group[0] * 2 * chips + 2 * chip
        rows = [got[first + core].astype(F32) for core in range(2)]
        sent[chip, shard + depth :, :] = jnp.concatenate(rows, axis=0).astype(BF16)


def tokens_kernel(counts, got, tokens, occupancy, grad_tokens):
    chips, (shard, width) = got.shape[0], tokens.shape
    normal, inverse = layer_norm(tokens[...].astype(F32))
    grad_normal = got[0, :shard, :].astype(F32)
    for chip in range(1, chips):
        grad_normal += got[chip, :shard, :].astype(F32)
    live = live_rows(occupancy[...], counts[0, 0], width)
    grad_normal = jnp.where(live > 0.0, grad_normal, 0.0)
    grad_input = inverse * (
        grad_normal
        - jnp.mean(grad_normal, axis=-1, keepdims=True)
        - normal * jnp.mean(grad_normal * normal, axis=-1, keepdims=True)
    )
    grad_tokens[...] = grad_input.astype(BF16)


def finish_kernel(core, got, other, query_rows, key_total, value_total):
    chips, depth, rows = got.shape[0], key_total.shape[0], query_rows.shape[0]
    shard = got.shape[1] - depth - 2 * rows

    def write(low, high):
        for chip in range(chips):
            for at, source in ((2 * chip, low), (2 * chip + 1, high)):
                cols = slice(at * HEAD, (at + 1) * HEAD)
                both = source[chip, shard : shard + depth, :].astype(F32)
                key_total[:, cols] = both[:, :HEAD]
                value_total[:, cols] = both[:, HEAD:]
                piece = source[chip, shard + depth :, :].astype(F32)
                both_rows = piece[:, HEAD:]
                query_rows[:, cols] = jnp.where(core[0] == 0, both_rows[:rows], both_rows[rows:])

    @pl.when(core[0] == 0)
    def _():
        write(got, other)

    @pl.when(core[0] != 0)
    def _():
        write(other, got)


def swap(array, axis):
    return lax.all_to_all(array, axis, 0, 0, tiled=True)


def shape(dims, dtype=BF16):
    return jax.ShapeDtypeStruct(dims, dtype)


def sibling(array):
    return lax.ppermute(array, "c", ((0, 1), (1, 0)))


def full(dims):
    return pl.BlockSpec(dims, lambda *_: (0,) * len(dims))


def column(dims, at):
    return pl.BlockSpec(dims, lambda step, heads: (0, heads[at]))


def body(tokens, occupancy, counts, queries, saved_lse, grad_out, attn_out, w_key, w_value):
    tokens, grad, out, lse = tokens[0], grad_out[0], attn_out[0], saved_lse[0]
    shard, width = tokens.shape
    latents, rows = queries.shape[0], grad.shape[0]
    chips, groups, windows = lax.axis_size("x"), lax.axis_size("z"), lax.axis_size("y")
    heads = lse.shape[1]
    core = lax.axis_index("c").astype(jnp.int32)
    head = (2 * lax.axis_index("x").astype(jnp.int32) + core).reshape(1)
    core, group = core.reshape(1), lax.axis_index("z").astype(jnp.int32).reshape(1)
    tokens, head, core, group = lax.optimization_barrier((tokens, head, core, group))
    sent = pl.pallas_call(
        pack_kernel,
        out_shape=shape((chips, shard + 2 * rows, width)),
        in_specs=[pl.BlockSpec(memory_space=pltpu.HBM)] * 6,
        out_specs=VMEM,
        scratch_shapes=[pltpu.SMEM(counts.shape, counts.dtype)]
        + [pltpu.VMEM(ref.shape, ref.dtype) for ref in (tokens, occupancy, grad, out, lse)]
        + [pltpu.SemaphoreType.DMA((6,))],
        compiler_params=params(60),
    )(counts, tokens, occupancy, grad, out, lse)
    got = swap(sent, "x")
    other = sibling(got)
    grads = pl.pallas_call(
        turn_kernel,
        out_shape=shape((2 * groups, rows * chips, width)),
        in_specs=[VMEM],
        out_specs=VMEM,
        compiler_params=params(8),
    )(got)
    grads = swap(grads, ("z", "c"))

    back = (chips, shard, width)
    part = (groups * windows, ROWS, width)
    sums = ((HEAD, latents), (width, width))
    many = (chips * shard, width)
    held = [pltpu.VMEM(many, BF16)] * 2 + [pltpu.SemaphoreType.DMA((chips * shard // BLOCK,))]
    work = pl.CostEstimate(
        flops=11 * chips * shard * latents * HEAD,
        bytes_accessed=4 * chips * shard * width,
        transcendentals=chips * shard * latents,
    )
    operands = [
        column((latents, HEAD), 0),
        column((width, HEAD), 0),
        column((width, HEAD), 0),
    ]
    rest = ((latents, HEAD), (ROWS, latents)) + sums
    keep, grad_rows, lines, *totals = pl.pallas_call(
        first_kernel,
        out_shape=(pltpu.HBM(many, BF16), shape(rest[0])) + tuple(shape(dims, F32) for dims in rest[1:]),
        grid_spec=pltpu.PrefetchScalarGridSpec(
            num_scalar_prefetch=1,
            grid=(1,),
            in_specs=[full(got.shape), full(grads.shape)] + operands,
            out_specs=[HBM] + [full(dims) for dims in rest],
            scratch_shapes=held,
        ),
        compiler_params=params(30),
        cost_estimate=work,
    )(head, got, grads, queries, w_key, w_value)
    give, parts = pl.pallas_call(
        second_kernel,
        out_shape=(pltpu.HBM(many, BF16), shape(part)),
        grid_spec=pltpu.PrefetchScalarGridSpec(
            num_scalar_prefetch=1,
            grid=(1,),
            in_specs=[full(other.shape)] + [full(dims) for dims in rest] + operands,
            out_specs=[HBM, full(part)],
            scratch_shapes=[pltpu.VMEM(sums[0], F32)] + held,
        ),
        compiler_params=params(30),
        cost_estimate=work,
    )(head, other, grad_rows, lines, *totals, queries, w_key, w_value)

    kept, given = pl.pallas_call(
        share_kernel,
        out_shape=(shape(back, F32), shape(back)),
        grid_spec=pltpu.PrefetchScalarGridSpec(
            num_scalar_prefetch=1,
            grid=(1,),
            in_specs=[full(many)] * 2 + [column((width, HEAD), 0)] * 2,
            out_specs=[full(back)] * 2,
        ),
        compiler_params=params(20),
        cost_estimate=pl.CostEstimate(flops=270000000, bytes_accessed=3000000, transcendentals=0),
    )(head, keep, give, w_key, w_value)
    theirs = sibling(given)
    parts = swap(parts, ("z", "y"))
    parts = pl.pallas_call(
        spread_kernel,
        out_shape=shape(part),
        in_specs=[VMEM],
        out_specs=VMEM,
        compiler_params=params(8),
    )(parts)
    parts = swap(parts, ("z", "y"))
    last = (chips, shard + width + 2 * rows, width)
    sent = pl.pallas_call(
        gather_kernel,
        out_shape=shape(last),
        in_specs=[SMEM] + [VMEM] * 3,
        out_specs=VMEM,
        compiler_params=params(16),
    )(group, kept, theirs, parts)
    got = swap(sent, "x")
    other = sibling(got)
    grad_tokens = pl.pallas_call(
        tokens_kernel,
        out_shape=shape((shard, width)),
        in_specs=[SMEM] + [VMEM] * 3,
        out_specs=VMEM,
        compiler_params=params(16),
        cost_estimate=pl.CostEstimate(flops=2000000, bytes_accessed=1000000, transcendentals=256),
    )(counts, got, tokens, occupancy)
    query_rows, key_total, value_total = pl.pallas_call(
        finish_kernel,
        out_shape=(
            shape((rows, heads * HEAD), F32),
            shape((width, heads * HEAD), F32),
            shape((width, heads * HEAD), F32),
        ),
        in_specs=[SMEM] + [VMEM] * 2,
        out_specs=(VMEM,) * 3,
        compiler_params=params(16),
    )(core, got, other)
    return grad_tokens[None], query_rows, key_total, value_total


def solution(mesh):
    seq, dp = mesh.shape["seq"], mesh.shape["dp"]
    split = Mesh(mesh.devices.reshape(seq // 8, 4, 2, dp), ("z", "x", "c", "y"))
    both = ("z", "x", "c")
    rows = P("y", both, None)
    return jax.shard_map(
        body,
        mesh=split,
        in_specs=(rows, P("y", both), P("y", both), P(), rows, rows, rows, P(), P()),
        out_specs=(rows, P(both, None), P(), P()),
        check_vma=False,
    )
```

```python
import math

import jax
import jax.numpy as jnp
from jax import lax
from jax.experimental import pallas as pl
from jax.experimental.pallas import tpu as pltpu
from jax.sharding import Mesh
from jax.sharding import PartitionSpec as P

HEAD = 128
ROWS = 8
BLOCK = 512
EPS = 1e-05
LOG2E = math.log2(math.e)
F32, BF16 = jnp.float32, jnp.bfloat16
VMEM = pl.BlockSpec(memory_space=pltpu.VMEM)
SMEM = pl.BlockSpec(memory_space=pltpu.SMEM)


def params(mib):
    return pltpu.CompilerParams(vmem_limit_bytes=mib * 1024 * 1024)


def mm(left, right, left_dim, right_dim):
    return lax.dot_general(
        left, right, (((left_dim,), (right_dim,)), ((), ())), preferred_element_type=F32
    )


def layer_norm(tokens):
    center = tokens - jnp.mean(tokens, axis=-1, keepdims=True)
    inverse = lax.rsqrt(jnp.mean(center * center, axis=-1, keepdims=True) + EPS)
    return center * inverse, inverse


def live_rows(occupancy, count, width):
    shard = occupancy.shape[1]
    place = lax.broadcasted_iota(jnp.int32, (1, shard), 1)
    live = jnp.where(place < count, occupancy, 0).astype(F32)
    return jnp.broadcast_to(live, (width, shard)).T


def three_parts(column):
    parts = []
    for _ in range(3):
        part = column.astype(BF16).astype(F32)
        parts.append(part)
        column = column - part
    return parts


def columns_of(head):
    return pl.ds(pl.multiple_of(head[0] * HEAD, HEAD), HEAD)


def pack_kernel(*refs):
    sources, sent, (counts, tokens, occupancy, grad, out, lse), done = (
        refs[:6],
        refs[6],
        refs[7:13],
        refs[13],
    )
    copies = [
        pltpu.make_async_copy(source, target, done.at[at])
        for at, (source, target) in enumerate(zip(sources, refs[7:13]))
    ]
    for copy in copies:
        copy.start()
    for copy in copies:
        copy.wait()
    chips, (shard, width) = sent.shape[0], tokens.shape
    live = live_rows(occupancy[...], counts[0, 0], width)
    masked = jnp.where(live > 0.0, tokens[...].astype(F32), 0.0).astype(BF16)
    rows = grad.shape[0]
    lane = lax.broadcasted_iota(jnp.int32, (rows, HEAD), 1)
    for chip in range(chips):
        sent[chip, :shard, :] = masked
        extras, grads = [], []
        for head in (2 * chip, 2 * chip + 1):
            cols = slice(head * HEAD, (head + 1) * HEAD)
            grad_f32 = grad[:, cols].astype(F32)
            delta = jnp.sum(grad_f32 * out[:, cols].astype(F32), axis=1, keepdims=True)
            extra = jnp.zeros((rows, HEAD), F32)
            for at, part in enumerate(three_parts(lse[:, head : head + 1]) + three_parts(delta)):
                extra = jnp.where(lane == at, part, extra)
            extras.append(extra)
            grads.append(grad_f32)
        both = jnp.concatenate(
            [jnp.concatenate(grads, axis=1), jnp.concatenate(extras, axis=1)], axis=0
        )
        sent[chip, shard:, :] = both.astype(BF16)


def turn_kernel(got, sent):
    chips, width = got.shape[0], got.shape[2]
    shard = got.shape[1] - sent.shape[1] // chips * 2
    pieces = [got[chip, shard:, :].astype(F32) for chip in range(chips)]
    rows = sent.shape[1] // chips
    grads = jnp.concatenate([piece[:rows] for piece in pieces], axis=0)
    extras = jnp.concatenate([piece[rows:] for piece in pieces], axis=0)
    for core in range(2):
        cols = slice(core * HEAD, (core + 1) * HEAD)
        both = jnp.concatenate([grads[:, cols], extras[:, cols]], axis=1).astype(BF16)
        for group in range(sent.shape[0] // 2):
            sent[2 * group + core] = both


def latent_order(got, chips):
    rows = got.shape[1] // chips
    blocks = [got[at].astype(F32) for at in range(got.shape[0])]
    return jnp.concatenate(
        [
            blocks[2 * group + core][chip * rows : (chip + 1) * rows]
            for group in range(got.shape[0] // 2)
            for chip in range(chips)
            for core in range(2)
        ],
        axis=0,
    )


def share_kernel(head, keep, give, w_key, w_value, kept, given):
    cols = columns_of(head)
    weights = jnp.concatenate([w_key[:, cols], w_value[:, cols]], axis=1)
    for chip in range(keep.shape[0]):
        kept[chip] = mm(keep[chip], weights, 1, 1)
        given[chip] = mm(give[chip], weights, 1, 1).astype(BF16)


def main_kernel(
    head, mine, other, got, query, w_key, w_value, keep, give, parts, query_sum, normals, grads
):
    cols = columns_of(head)
    chips, shard = keep.shape[0], keep.shape[1]
    scale = 1.0 / math.sqrt(HEAD)
    rows = latent_order(got, chips)
    grad = rows[:, :HEAD].astype(BF16)
    extra = rows[:, HEAD:].T
    lse = (extra[0:1] + extra[1:2] + extra[2:3]) * LOG2E
    delta = extra[3:4] + extra[4:5] + extra[5:6]
    queries = query[:, cols]
    weights = jnp.concatenate([w_key[:, cols], w_value[:, cols]], axis=1)
    per = BLOCK // shard
    for block in range(2 * chips // per):
        first = block * per
        source, target = (mine, keep) if first < chips else (other, give)
        spots = [(first + at) % chips for at in range(per)]
        tokens = jnp.concatenate([source[spot, :shard, :] for spot in spots], axis=0)
        normal = layer_norm(tokens.astype(F32))[0].astype(BF16)
        both = jnp.dot(normal, weights, preferred_element_type=F32).astype(BF16)
        keys, values = both[:, :HEAD], both[:, HEAD:]
        probs = jnp.exp2(mm(keys, queries, 1, 1) * (scale * LOG2E) - lse)
        grad_values = jnp.dot(probs.astype(BF16), grad, preferred_element_type=F32)
        grad_probs = mm(values, grad, 1, 1)
        grad_scores = (scale * probs * (grad_probs - delta)).astype(BF16)
        grad_keys = jnp.dot(grad_scores, queries, preferred_element_type=F32)
        grad_both = jnp.concatenate([grad_keys, grad_values], axis=1).astype(BF16)
        for at, spot in enumerate(spots):
            target[spot] = grad_both[at * shard : (at + 1) * shard]
        query_part = mm(keys, grad_scores, 0, 0)
        if block == 0:
            query_sum[...] = query_part
        else:
            query_sum[...] += query_part
        normals[block * BLOCK : (block + 1) * BLOCK, :] = normal
        grads[block * BLOCK : (block + 1) * BLOCK, :] = grad_both
    turned = query_sum[...].T
    totals = mm(normals[...], grads[...], 0, 0)
    halves = parts.shape[0] // 2
    for at in range(parts.shape[0]):
        start = at % halves * ROWS
        cols = slice(at // halves * HEAD, (at // halves + 1) * HEAD)
        piece = [totals[start : start + ROWS, cols], turned[at * ROWS : (at + 1) * ROWS]]
        parts[at] = jnp.concatenate(piece, axis=1).astype(BF16)


def add_up(got):
    total = got[0].astype(F32)
    for at in range(1, got.shape[0]):
        total = total + got[at].astype(F32)
    return total


def spread_kernel(got, sent):
    total = add_up(got).astype(BF16)
    for at in range(sent.shape[0]):
        sent[at] = total


def combine_kernel(chip, kept, theirs, *shares):
    chips = kept.shape[0]
    for ahead in range(chips):
        at = lax.rem(chip[0] + ahead, chips)
        shares[ahead][...] = (kept[at] + theirs[at].astype(F32)).astype(BF16)


def gather_kernel(group, got, sent):
    chips = sent.shape[0]
    halves = got.shape[0] // 2
    depth = halves * ROWS
    pieces = [got[at].astype(F32)[:, :HEAD] for at in range(2 * halves)]
    weights = jnp.concatenate(
        [jnp.concatenate(pieces[:halves], axis=0), jnp.concatenate(pieces[halves:], axis=0)], axis=1
    ).astype(BF16)
    for chip in range(chips):
        sent[chip, :depth, :] = weights
        first = group[0] * 2 * chips + 2 * chip
        rows = [got[first + core].astype(F32) for core in range(2)]
        sent[chip, depth:, :] = jnp.concatenate(rows, axis=0).astype(BF16)


def tokens_kernel(counts, *refs):
    shares, (tokens, occupancy, grad_tokens) = refs[:-3], refs[-3:]
    width = tokens.shape[1]
    normal, inverse = layer_norm(tokens[...].astype(F32))
    grad_normal = shares[0][...].astype(F32)
    for share in shares[1:]:
        grad_normal += share[...].astype(F32)
    live = live_rows(occupancy[...], counts[0, 0], width)
    grad_normal = jnp.where(live > 0.0, grad_normal, 0.0)
    grad_input = inverse * (
        grad_normal
        - jnp.mean(grad_normal, axis=-1, keepdims=True)
        - normal * jnp.mean(grad_normal * normal, axis=-1, keepdims=True)
    )
    grad_tokens[...] = grad_input.astype(BF16)


def finish_kernel(core, got, other, query_rows, key_total, value_total):
    chips, depth, rows = got.shape[0], key_total.shape[0], query_rows.shape[0]
    def write(low, high):
        for chip in range(chips):
            for at, source in ((2 * chip, low), (2 * chip + 1, high)):
                cols = slice(at * HEAD, (at + 1) * HEAD)
                both = source[chip, :depth, :].astype(F32)
                key_total[:, cols] = both[:, :HEAD]
                value_total[:, cols] = both[:, HEAD:]
                piece = source[chip, depth:, :].astype(F32)
                both_rows = piece[:, HEAD:]
                query_rows[:, cols] = jnp.where(core[0] == 0, both_rows[:rows], both_rows[rows:])

    @pl.when(core[0] == 0)
    def _():
        write(got, other)

    @pl.when(core[0] != 0)
    def _():
        write(other, got)


def swap(array, axis):
    return lax.all_to_all(array, axis, 0, 0, tiled=True)


def shape(dims, dtype=BF16):
    return jax.ShapeDtypeStruct(dims, dtype)


def sibling(array):
    return lax.ppermute(array, "c", ((0, 1), (1, 0)))


def body(tokens, occupancy, counts, queries, saved_lse, grad_out, attn_out, w_key, w_value):
    tokens, grad, out, lse = tokens[0], grad_out[0], attn_out[0], saved_lse[0]
    shard, width = tokens.shape
    latents, rows = queries.shape[0], grad.shape[0]
    chips, groups, windows = lax.axis_size("x"), lax.axis_size("z"), lax.axis_size("y")
    heads = lse.shape[1]
    core, chip, group = (lax.axis_index(at).astype(jnp.int32) for at in ("c", "x", "z"))
    head = (2 * chip + core).reshape(1)
    core, chip, group = core.reshape(1), chip.reshape(1), group.reshape(1)
    tokens, head, core, chip, group = lax.optimization_barrier((tokens, head, core, chip, group))
    sent = pl.pallas_call(
        pack_kernel,
        out_shape=shape((chips, shard + 2 * rows, width)),
        in_specs=[pl.BlockSpec(memory_space=pltpu.HBM)] * 6,
        out_specs=VMEM,
        scratch_shapes=[pltpu.SMEM(counts.shape, counts.dtype)]
        + [pltpu.VMEM(ref.shape, ref.dtype) for ref in (tokens, occupancy, grad, out, lse)]
        + [pltpu.SemaphoreType.DMA((6,))],
        compiler_params=params(60),
    )(counts, tokens, occupancy, grad, out, lse)
    got = swap(sent, "x")
    other = sibling(got)
    grads = pl.pallas_call(
        turn_kernel,
        out_shape=shape((2 * groups, rows * chips, width)),
        in_specs=[VMEM],
        out_specs=VMEM,
        compiler_params=params(8),
    )(got)
    grads = swap(grads, ("z", "c"))

    back = (chips, shard, width)
    part = (groups * windows, ROWS, width)
    many = (2 * chips * shard, width)
    keep, give, parts = pl.pallas_call(
        main_kernel,
        out_shape=(shape(back), shape(back), shape(part)),
        in_specs=[SMEM] + [VMEM] * 6,
        out_specs=(VMEM,) * 3,
        scratch_shapes=[pltpu.VMEM((HEAD, latents), F32)] + [pltpu.VMEM(many, BF16)] * 2,
        compiler_params=params(40),
    )(head, got, other, grads, queries, w_key, w_value)
    kept, given = pl.pallas_call(
        share_kernel,
        out_shape=(shape(back, F32), shape(back)),
        in_specs=[SMEM] + [VMEM] * 4,
        out_specs=(VMEM,) * 2,
        compiler_params=params(16),
        cost_estimate=pl.CostEstimate(flops=270000000, bytes_accessed=3000000, transcendentals=0),
    )(head, keep, give, w_key, w_value)
    shares = pl.pallas_call(
        combine_kernel,
        out_shape=(shape((shard, width)),) * chips,
        in_specs=[SMEM] + [VMEM] * 2,
        out_specs=(VMEM,) * chips,
        compiler_params=params(16),
    )(chip, kept, sibling(given))
    shares = [shares[0]] + [
        lax.ppermute(share, "x", [(at, (at + ahead) % chips) for at in range(chips)])
        for ahead, share in enumerate(shares[1:], 1)
    ]
    parts = swap(parts, ("z", "y"))
    parts = pl.pallas_call(
        spread_kernel,
        out_shape=shape(part),
        in_specs=[VMEM],
        out_specs=VMEM,
        compiler_params=params(8),
    )(parts)
    parts = swap(parts, ("z", "y"))
    last = (chips, width + 2 * rows, width)
    sent = pl.pallas_call(
        gather_kernel,
        out_shape=shape(last),
        in_specs=[SMEM, VMEM],
        out_specs=VMEM,
        compiler_params=params(16),
    )(group, parts)
    sent, *shares = lax.optimization_barrier((sent, *shares))
    got = swap(sent, "x")
    other = sibling(got)
    grad_tokens = pl.pallas_call(
        tokens_kernel,
        out_shape=shape((shard, width)),
        in_specs=[SMEM] + [VMEM] * (chips + 2),
        out_specs=VMEM,
        compiler_params=params(16),
        cost_estimate=pl.CostEstimate(flops=2000000, bytes_accessed=1000000, transcendentals=256),
    )(counts, *shares, tokens, occupancy)
    query_rows, key_total, value_total = pl.pallas_call(
        finish_kernel,
        out_shape=(
            shape((rows, heads * HEAD), F32),
            shape((width, heads * HEAD), F32),
            shape((width, heads * HEAD), F32),
        ),
        in_specs=[SMEM] + [VMEM] * 2,
        out_specs=(VMEM,) * 3,
        compiler_params=params(16),
    )(core, got, other)
    return grad_tokens[None], query_rows, key_total, value_total


def solution(mesh):
    seq, dp = mesh.shape["seq"], mesh.shape["dp"]
    split = Mesh(mesh.devices.reshape(seq // 8, 4, 2, dp), ("z", "x", "c", "y"))
    both = ("z", "x", "c")
    rows = P("y", both, None)
    return jax.shard_map(
        body,
        mesh=split,
        in_specs=(rows, P("y", both), P("y", both), P(), rows, rows, rows, P(), P()),
        out_specs=(rows, P(both, None), P(), P()),
        check_vma=False,
    )
```

```python
import math

import jax
import jax.numpy as jnp
from jax import lax
from jax.experimental import pallas as pl
from jax.experimental.pallas import tpu as pltpu
from jax.sharding import Mesh
from jax.sharding import PartitionSpec as P

HEAD = 128
ROWS = 8
BLOCK = 512
EPS = 1e-05
LOG2E = math.log2(math.e)
F32, BF16 = jnp.float32, jnp.bfloat16
VMEM = pl.BlockSpec(memory_space=pltpu.VMEM)
HBM = pl.BlockSpec(memory_space=pltpu.HBM)
SMEM = pl.BlockSpec(memory_space=pltpu.SMEM)


def params(mib):
    return pltpu.CompilerParams(vmem_limit_bytes=mib * 1024 * 1024)


def mm(left, right, left_dim, right_dim):
    return lax.dot_general(
        left, right, (((left_dim,), (right_dim,)), ((), ())), preferred_element_type=F32
    )


def layer_norm(tokens):
    center = tokens - jnp.mean(tokens, axis=-1, keepdims=True)
    inverse = lax.rsqrt(jnp.mean(center * center, axis=-1, keepdims=True) + EPS)
    return center * inverse, inverse


def live_rows(occupancy, count, width):
    shard = occupancy.shape[1]
    place = lax.broadcasted_iota(jnp.int32, (1, shard), 1)
    live = jnp.where(place < count, occupancy, 0).astype(F32)
    return jnp.broadcast_to(live, (width, shard)).T


def three_parts(column):
    parts = []
    for _ in range(3):
        part = column.astype(BF16).astype(F32)
        parts.append(part)
        column = column - part
    return parts


def columns_of(head):
    return pl.ds(pl.multiple_of(head[0] * HEAD, HEAD), HEAD)


def pack_kernel(*refs):
    sources, (masked, sent), held, done = refs[:6], refs[6:8], refs[8:14], refs[14]
    copies = [
        pltpu.make_async_copy(source, target, done.at[at])
        for at, (source, target) in enumerate(zip(sources, held))
    ]
    for copy in copies:
        copy.start()
    for copy in copies:
        copy.wait()
    counts, tokens, occupancy, grad, out, lse = held
    live = live_rows(occupancy[...], counts[0, 0], tokens.shape[1])
    masked[...] = jnp.where(live > 0.0, tokens[...].astype(F32), 0.0).astype(BF16)
    rows, heads = grad.shape[0], lse.shape[1]
    lane = lax.broadcasted_iota(jnp.int32, (rows, HEAD), 1)
    for head in range(heads):
        cols = slice(head * HEAD, (head + 1) * HEAD)
        grad_f32 = grad[:, cols].astype(F32)
        delta = jnp.sum(grad_f32 * out[:, cols].astype(F32), axis=1, keepdims=True)
        extra = jnp.zeros((rows, HEAD), F32)
        for at, part in enumerate(three_parts(lse[:, head : head + 1]) + three_parts(delta)):
            extra = jnp.where(lane == at, part, extra)
        both = jnp.concatenate([grad_f32, extra], axis=1).astype(BF16)
        for group in range(sent.shape[0] // heads):
            sent[group * heads + head] = both


def normal_kernel(*refs):
    blocks, normals = refs[:-1], refs[-1]
    shard = blocks[0].shape[0]
    for at, block in enumerate(blocks):
        normal = layer_norm(block[...].astype(F32))[0].astype(BF16)
        normals[at * shard : (at + 1) * shard, :] = normal


def share_kernel(head, keep, give, w_key, w_value, kept, given):
    cols = columns_of(head)
    weights = jnp.concatenate([w_key[:, cols], w_value[:, cols]], axis=1)
    kept[...] = mm(keep[...], weights, 1, 1)
    given[...] = mm(give[...], weights, 1, 1).astype(BF16)


def main_kernel(head, mine, other, got, query, w_key, w_value, keep, give, parts, query_sum):
    cols = columns_of(head)
    scale = 1.0 / math.sqrt(HEAD)
    grad = got[:, :HEAD]
    extra = got[:, HEAD:].astype(F32).T
    lse = (extra[0:1] + extra[1:2] + extra[2:3]) * LOG2E
    delta = extra[3:4] + extra[4:5] + extra[5:6]
    queries = query[:, cols]
    weights = jnp.concatenate([w_key[:, cols], w_value[:, cols]], axis=1)
    for source, target in ((mine, keep), (other, give)):
        for start in range(0, source.shape[0], BLOCK):
            rows = slice(start, start + BLOCK)
            both = jnp.dot(source[rows, :], weights, preferred_element_type=F32).astype(BF16)
            keys, values = both[:, :HEAD], both[:, HEAD:]
            probs = jnp.exp2(mm(keys, queries, 1, 1) * (scale * LOG2E) - lse)
            grad_values = jnp.dot(probs.astype(BF16), grad, preferred_element_type=F32)
            grad_probs = mm(values, grad, 1, 1)
            grad_scores = (scale * probs * (grad_probs - delta)).astype(BF16)
            grad_keys = jnp.dot(grad_scores, queries, preferred_element_type=F32)
            target[rows, :] = jnp.concatenate([grad_keys, grad_values], axis=1).astype(BF16)
            query_part = mm(keys, grad_scores, 0, 0)
            if source is mine and start == 0:
                query_sum[...] = query_part
            else:
                query_sum[...] += query_part
    totals = mm(mine[...], keep[...], 0, 0) + mm(other[...], give[...], 0, 0)
    turned = query_sum[...].T
    halves = parts.shape[0] // 2
    for at in range(parts.shape[0]):
        start = at % halves * ROWS
        cols = slice(at // halves * HEAD, (at // halves + 1) * HEAD)
        piece = [totals[start : start + ROWS, cols], turned[at * ROWS : (at + 1) * ROWS]]
        parts[at] = jnp.concatenate(piece, axis=1).astype(BF16)


def add_up(got):
    total = got[0].astype(F32)
    for at in range(1, got.shape[0]):
        total = total + got[at].astype(F32)
    return total


def spread_kernel(got, sent):
    total = add_up(got).astype(BF16)
    for at in range(sent.shape[0]):
        sent[at] = total


def combine_kernel(kept, theirs, *shares):
    chips, shard = len(shares), shares[0].shape[0]
    for ahead in range(chips):
        at = (chips - ahead) % chips * shard
        rows = slice(at, at + shard)
        shares[ahead][...] = (kept[rows, :] + theirs[rows, :].astype(F32)).astype(BF16)


def gather_kernel(group, got, sent):
    chips = sent.shape[0]
    halves = got.shape[0] // 2
    depth = halves * ROWS
    pieces = [got[at].astype(F32)[:, :HEAD] for at in range(2 * halves)]
    weights = jnp.concatenate(
        [jnp.concatenate(pieces[:halves], axis=0), jnp.concatenate(pieces[halves:], axis=0)], axis=1
    ).astype(BF16)
    for chip in range(chips):
        sent[chip, :depth, :] = weights
        first = group[0] * 2 * chips + 2 * chip
        rows = [got[first + core].astype(F32) for core in range(2)]
        sent[chip, depth:, :] = jnp.concatenate(rows, axis=0).astype(BF16)


def tokens_kernel(counts, *refs):
    shares, (tokens, occupancy, grad_tokens) = refs[:-3], refs[-3:]
    width = tokens.shape[1]
    normal, inverse = layer_norm(tokens[...].astype(F32))
    grad_normal = shares[0][...].astype(F32)
    for share in shares[1:]:
        grad_normal += share[...].astype(F32)
    live = live_rows(occupancy[...], counts[0, 0], width)
    grad_normal = jnp.where(live > 0.0, grad_normal, 0.0)
    grad_input = inverse * (
        grad_normal
        - jnp.mean(grad_normal, axis=-1, keepdims=True)
        - normal * jnp.mean(grad_normal * normal, axis=-1, keepdims=True)
    )
    grad_tokens[...] = grad_input.astype(BF16)


def finish_kernel(core, got, other, query_rows, key_total, value_total):
    chips, depth, rows = got.shape[0], key_total.shape[0], query_rows.shape[0]
    def write(low, high):
        for chip in range(chips):
            for at, source in ((2 * chip, low), (2 * chip + 1, high)):
                cols = slice(at * HEAD, (at + 1) * HEAD)
                both = source[chip, :depth, :].astype(F32)
                key_total[:, cols] = both[:, :HEAD]
                value_total[:, cols] = both[:, HEAD:]
                piece = source[chip, depth:, :].astype(F32)
                both_rows = piece[:, HEAD:]
                query_rows[:, cols] = jnp.where(core[0] == 0, both_rows[:rows], both_rows[rows:])

    @pl.when(core[0] == 0)
    def _():
        write(got, other)

    @pl.when(core[0] != 0)
    def _():
        write(other, got)


def swap(array, axis):
    return lax.all_to_all(array, axis, 0, 0, tiled=True)


def shape(dims, dtype=BF16):
    return jax.ShapeDtypeStruct(dims, dtype)


def sibling(array):
    return lax.ppermute(array, "c", ((0, 1), (1, 0)))


def along_x(array, ahead, chips):
    return lax.ppermute(array, "x", [(at, (at + ahead) % chips) for at in range(chips)])


def body(tokens, occupancy, counts, queries, saved_lse, grad_out, attn_out, w_key, w_value):
    tokens, grad, out, lse = tokens[0], grad_out[0], attn_out[0], saved_lse[0]
    shard, width = tokens.shape
    latents, rows = queries.shape[0], grad.shape[0]
    chips, groups, windows = lax.axis_size("x"), lax.axis_size("z"), lax.axis_size("y")
    heads = lse.shape[1]
    core, chip, group = (lax.axis_index(at).astype(jnp.int32) for at in ("c", "x", "z"))
    head = (2 * chip + core).reshape(1)
    core, group = core.reshape(1), group.reshape(1)
    tokens, head, core, group = lax.optimization_barrier((tokens, head, core, group))
    masked, sent = pl.pallas_call(
        pack_kernel,
        out_shape=(shape((shard, width)), shape((groups * heads, rows, width))),
        in_specs=[HBM] * 6,
        out_specs=(VMEM, VMEM),
        scratch_shapes=[pltpu.SMEM(counts.shape, counts.dtype)]
        + [pltpu.VMEM(ref.shape, ref.dtype) for ref in (tokens, occupancy, grad, out, lse)]
        + [pltpu.SemaphoreType.DMA((6,))],
        compiler_params=params(60),
    )(counts, tokens, occupancy, grad, out, lse)
    grads, masked, *blocks = lax.optimization_barrier(
        (
            swap(sent, ("z", "x", "c")),
            masked,
            *[along_x(masked, ahead, chips) for ahead in range(1, chips)],
        )
    )
    back = (chips * shard, width)
    normals = pl.pallas_call(
        normal_kernel,
        out_shape=shape(back),
        in_specs=[VMEM] * chips,
        out_specs=VMEM,
        compiler_params=params(8),
    )(masked, *blocks)
    other = sibling(normals)

    part = (groups * windows, ROWS, width)
    keep, give, parts = pl.pallas_call(
        main_kernel,
        out_shape=(shape(back), shape(back), shape(part)),
        in_specs=[SMEM] + [VMEM] * 6,
        out_specs=(VMEM,) * 3,
        scratch_shapes=[pltpu.VMEM((HEAD, latents), F32)],
        compiler_params=params(40),
    )(head, normals, other, grads.reshape(latents, width), queries, w_key, w_value)
    kept, given = pl.pallas_call(
        share_kernel,
        out_shape=(shape(back, F32), shape(back)),
        in_specs=[SMEM] + [VMEM] * 4,
        out_specs=(VMEM,) * 2,
        compiler_params=params(16),
        cost_estimate=pl.CostEstimate(flops=270000000, bytes_accessed=3000000, transcendentals=0),
    )(head, keep, give, w_key, w_value)
    shares = pl.pallas_call(
        combine_kernel,
        out_shape=(shape((shard, width)),) * chips,
        in_specs=[VMEM] * 2,
        out_specs=(VMEM,) * chips,
        compiler_params=params(16),
    )(kept, sibling(given))
    shares = [shares[0]] + [
        along_x(share, ahead, chips) for ahead, share in enumerate(shares[1:], 1)
    ]
    parts = swap(parts, ("z", "y"))
    parts = pl.pallas_call(
        spread_kernel,
        out_shape=shape(part),
        in_specs=[VMEM],
        out_specs=VMEM,
        compiler_params=params(8),
    )(parts)
    parts = swap(parts, ("z", "y"))
    last = (chips, width + 2 * rows, width)
    sent = pl.pallas_call(
        gather_kernel,
        out_shape=shape(last),
        in_specs=[SMEM, VMEM],
        out_specs=VMEM,
        compiler_params=params(16),
    )(group, parts)
    sent, *shares = lax.optimization_barrier((sent, *shares))
    got = swap(sent, "x")
    other = sibling(got)
    grad_tokens = pl.pallas_call(
        tokens_kernel,
        out_shape=shape((shard, width)),
        in_specs=[SMEM] + [VMEM] * (chips + 2),
        out_specs=VMEM,
        compiler_params=params(16),
        cost_estimate=pl.CostEstimate(flops=2000000, bytes_accessed=1000000, transcendentals=256),
    )(counts, *shares, tokens, occupancy)
    query_rows, key_total, value_total = pl.pallas_call(
        finish_kernel,
        out_shape=(
            shape((rows, heads * HEAD), F32),
            shape((width, heads * HEAD), F32),
            shape((width, heads * HEAD), F32),
        ),
        in_specs=[SMEM] + [VMEM] * 2,
        out_specs=(VMEM,) * 3,
        compiler_params=params(16),
    )(core, got, other)
    return grad_tokens[None], query_rows, key_total, value_total


def solution(mesh):
    seq, dp = mesh.shape["seq"], mesh.shape["dp"]
    split = Mesh(mesh.devices.reshape(seq // 8, 4, 2, dp), ("z", "x", "c", "y"))
    both = ("z", "x", "c")
    rows = P("y", both, None)
    return jax.shard_map(
        body,
        mesh=split,
        in_specs=(rows, P("y", both), P("y", both), P(), rows, rows, rows, P(), P()),
        out_specs=(rows, P(both, None), P(), P()),
        check_vma=False,
    )
```

```python
import math

import jax
import jax.numpy as jnp
from jax import lax
from jax.experimental import pallas as pl
from jax.experimental.pallas import tpu as pltpu
from jax.sharding import Mesh
from jax.sharding import PartitionSpec as P

HEAD = 128
ROWS = 8
BLOCK = 512
EPS = 1e-05
LOG2E = math.log2(math.e)
F32, BF16 = jnp.float32, jnp.bfloat16
VMEM = pl.BlockSpec(memory_space=pltpu.VMEM)
SMEM = pl.BlockSpec(memory_space=pltpu.SMEM)


def params(mib):
    return pltpu.CompilerParams(vmem_limit_bytes=mib * 1024 * 1024)


def mm(left, right, left_dim, right_dim):
    return lax.dot_general(
        left, right, (((left_dim,), (right_dim,)), ((), ())), preferred_element_type=F32
    )


def layer_norm(tokens):
    center = tokens - jnp.mean(tokens, axis=-1, keepdims=True)
    inverse = lax.rsqrt(jnp.mean(center * center, axis=-1, keepdims=True) + EPS)
    return center * inverse, inverse


def live_rows(occupancy, count, width):
    shard = occupancy.shape[1]
    place = lax.broadcasted_iota(jnp.int32, (1, shard), 1)
    live = jnp.where(place < count, occupancy, 0).astype(F32)
    return jnp.broadcast_to(live, (width, shard)).T


def three_parts(column):
    parts = []
    for _ in range(3):
        part = column.astype(BF16).astype(F32)
        parts.append(part)
        column = column - part
    return parts


def columns_of(head):
    return pl.ds(pl.multiple_of(head[0] * HEAD, HEAD), HEAD)


def pack_kernel(*refs):
    sources, sent, (counts, tokens, occupancy, grad, out, lse), done = (
        refs[:6],
        refs[6],
        refs[7:13],
        refs[13],
    )
    copies = [
        pltpu.make_async_copy(source, target, done.at[at])
        for at, (source, target) in enumerate(zip(sources, refs[7:13]))
    ]
    for copy in copies:
        copy.start()
    for copy in copies:
        copy.wait()
    chips, (shard, width) = sent.shape[0], tokens.shape
    live = live_rows(occupancy[...], counts[0, 0], width)
    masked = jnp.where(live > 0.0, tokens[...].astype(F32), 0.0).astype(BF16)
    rows = grad.shape[0]
    lane = lax.broadcasted_iota(jnp.int32, (rows, HEAD), 1)
    for chip in range(chips):
        sent[chip, :shard, :] = masked
        extras, grads = [], []
        for head in (2 * chip, 2 * chip + 1):
            cols = slice(head * HEAD, (head + 1) * HEAD)
            grad_f32 = grad[:, cols].astype(F32)
            delta = jnp.sum(grad_f32 * out[:, cols].astype(F32), axis=1, keepdims=True)
            extra = jnp.zeros((rows, HEAD), F32)
            for at, part in enumerate(three_parts(lse[:, head : head + 1]) + three_parts(delta)):
                extra = jnp.where(lane == at, part, extra)
            extras.append(extra)
            grads.append(grad_f32)
        both = jnp.concatenate(
            [jnp.concatenate(grads, axis=1), jnp.concatenate(extras, axis=1)], axis=0
        )
        sent[chip, shard:, :] = both.astype(BF16)


def turn_kernel(got, sent):
    chips, width = got.shape[0], got.shape[2]
    shard = got.shape[1] - sent.shape[1] // chips * 2
    pieces = [got[chip, shard:, :].astype(F32) for chip in range(chips)]
    rows = sent.shape[1] // chips
    grads = jnp.concatenate([piece[:rows] for piece in pieces], axis=0)
    extras = jnp.concatenate([piece[rows:] for piece in pieces], axis=0)
    for core in range(2):
        cols = slice(core * HEAD, (core + 1) * HEAD)
        both = jnp.concatenate([grads[:, cols], extras[:, cols]], axis=1).astype(BF16)
        for group in range(sent.shape[0] // 2):
            sent[2 * group + core] = both


def latent_order(got, chips):
    rows = got.shape[1] // chips
    blocks = [got[at].astype(F32) for at in range(got.shape[0])]
    return jnp.concatenate(
        [
            blocks[2 * group + core][chip * rows : (chip + 1) * rows]
            for group in range(got.shape[0] // 2)
            for chip in range(chips)
            for core in range(2)
        ],
        axis=0,
    )


def share_kernel(head, keep, give, w_key, w_value, kept, given):
    cols = columns_of(head)
    weights = jnp.concatenate([w_key[:, cols], w_value[:, cols]], axis=1)
    for chip in range(keep.shape[0]):
        kept[chip] = mm(keep[chip], weights, 1, 1)
        given[chip] = mm(give[chip], weights, 1, 1).astype(BF16)


def main_kernel(
    head, mine, other, got, query, w_key, w_value, keep, give, parts, query_sum, normals, grads
):
    cols = columns_of(head)
    chips, shard = keep.shape[0], keep.shape[1]
    scale = 1.0 / math.sqrt(HEAD)
    rows = latent_order(got, chips)
    grad = rows[:, :HEAD].astype(BF16)
    extra = rows[:, HEAD:].T
    lse = (extra[0:1] + extra[1:2] + extra[2:3]) * LOG2E
    delta = extra[3:4] + extra[4:5] + extra[5:6]
    queries = query[:, cols]
    weights = jnp.concatenate([w_key[:, cols], w_value[:, cols]], axis=1)
    per = BLOCK // shard
    for block in range(2 * chips // per):
        first = block * per
        source, target = (mine, keep) if first < chips else (other, give)
        spots = [(first + at) % chips for at in range(per)]
        tokens = jnp.concatenate([source[spot, :shard, :] for spot in spots], axis=0)
        normal = layer_norm(tokens.astype(F32))[0].astype(BF16)
        both = jnp.dot(normal, weights, preferred_element_type=F32).astype(BF16)
        keys, values = both[:, :HEAD], both[:, HEAD:]
        probs = jnp.exp2(mm(keys, queries, 1, 1) * (scale * LOG2E) - lse)
        grad_values = jnp.dot(probs.astype(BF16), grad, preferred_element_type=F32)
        grad_probs = mm(values, grad, 1, 1)
        grad_scores = (scale * probs * (grad_probs - delta)).astype(BF16)
        grad_keys = jnp.dot(grad_scores, queries, preferred_element_type=F32)
        grad_both = jnp.concatenate([grad_keys, grad_values], axis=1).astype(BF16)
        for at, spot in enumerate(spots):
            target[spot] = grad_both[at * shard : (at + 1) * shard]
        query_part = mm(keys, grad_scores, 0, 0)
        if block == 0:
            query_sum[...] = query_part
        else:
            query_sum[...] += query_part
        normals[block * BLOCK : (block + 1) * BLOCK, :] = normal
        grads[block * BLOCK : (block + 1) * BLOCK, :] = grad_both
    turned = query_sum[...].T.astype(BF16)
    totals = mm(normals[...], grads[...], 0, 0).astype(BF16)
    groups, part_rows = parts.shape[0], parts.shape[1]
    each = totals.shape[0] // groups
    half = part_rows - each
    for group in range(groups):
        parts[group, :each, :] = totals[group * each : (group + 1) * each, :]
        start = group * 2 * half
        parts[group, each:, :HEAD] = turned[start : start + half]
        parts[group, each:, HEAD:] = turned[start + half : start + 2 * half]


def add_up(got):
    total = got[0].astype(F32)
    for at in range(1, got.shape[0]):
        total = total + got[at].astype(F32)
    return total


def spread_kernel(got, sent):
    total = add_up(got).astype(BF16)
    for at in range(sent.shape[0]):
        sent[at] = total


def total_kernel(got, sent, query_rows):
    total = add_up(got)
    each = sent.shape[1]
    low = total[:each].astype(BF16)
    for at in range(sent.shape[0]):
        sent[at] = low
    query_rows[: got.shape[1] - each, :] = total[each:, :HEAD]
    query_rows[got.shape[1] - each :, :] = total[each:, HEAD:]


def combine_kernel(chip, kept, theirs, *shares):
    chips = kept.shape[0]
    for ahead in range(chips):
        at = lax.rem(chip[0] + ahead, chips)
        shares[ahead][...] = (kept[at] + theirs[at].astype(F32)).astype(BF16)


def gather_kernel(weights, query_rows, sent):
    chips, depth = sent.shape[0], weights.shape[0]
    rows = query_rows.shape[0] // chips
    for chip in range(chips):
        sent[chip, :depth, :] = weights[...]
        piece = query_rows[chip * rows : (chip + 1) * rows, :]
        high = piece.astype(BF16).astype(F32)
        sent[chip, depth:, :] = jnp.concatenate([high, piece - high], axis=1).astype(BF16)


def tokens_kernel(counts, *refs):
    shares, (tokens, occupancy, grad_tokens) = refs[:-3], refs[-3:]
    width = tokens.shape[1]
    normal, inverse = layer_norm(tokens[...].astype(F32))
    grad_normal = shares[0][...].astype(F32)
    for share in shares[1:]:
        grad_normal += share[...].astype(F32)
    live = live_rows(occupancy[...], counts[0, 0], width)
    grad_normal = jnp.where(live > 0.0, grad_normal, 0.0)
    grad_input = inverse * (
        grad_normal
        - jnp.mean(grad_normal, axis=-1, keepdims=True)
        - normal * jnp.mean(grad_normal * normal, axis=-1, keepdims=True)
    )
    grad_tokens[...] = grad_input.astype(BF16)


def finish_kernel(core, got, other, query_rows, key_total, value_total):
    chips, depth, rows = got.shape[0], key_total.shape[0], query_rows.shape[0]
    def write(low, high):
        for chip in range(chips):
            for at, source in ((2 * chip, low), (2 * chip + 1, high)):
                cols = slice(at * HEAD, (at + 1) * HEAD)
                both = source[chip, :depth, :].astype(F32)
                key_total[:, cols] = both[:, :HEAD]
                value_total[:, cols] = both[:, HEAD:]
                piece = source[chip, depth:, :].astype(F32)
                both_rows = piece[:, :HEAD] + piece[:, HEAD:]
                query_rows[:, cols] = jnp.where(core[0] == 0, both_rows[:rows], both_rows[rows:])

    @pl.when(core[0] == 0)
    def _():
        write(got, other)

    @pl.when(core[0] != 0)
    def _():
        write(other, got)


def swap(array, axis):
    return lax.all_to_all(array, axis, 0, 0, tiled=True)


def shape(dims, dtype=BF16):
    return jax.ShapeDtypeStruct(dims, dtype)


def sibling(array):
    return lax.ppermute(array, "c", ((0, 1), (1, 0)))


def along_x(array, ahead, chips):
    return lax.ppermute(array, "x", [(at, (at + ahead) % chips) for at in range(chips)])


def body(tokens, occupancy, counts, queries, saved_lse, grad_out, attn_out, w_key, w_value):
    tokens, grad, out, lse = tokens[0], grad_out[0], attn_out[0], saved_lse[0]
    shard, width = tokens.shape
    latents, rows = queries.shape[0], grad.shape[0]
    chips, groups, windows = lax.axis_size("x"), lax.axis_size("z"), lax.axis_size("y")
    heads = lse.shape[1]
    core, chip = (lax.axis_index(at).astype(jnp.int32) for at in ("c", "x"))
    head = (2 * chip + core).reshape(1)
    core, chip = core.reshape(1), chip.reshape(1)
    tokens, head, core, chip = lax.optimization_barrier((tokens, head, core, chip))
    sent = pl.pallas_call(
        pack_kernel,
        out_shape=shape((chips, shard + 2 * rows, width)),
        in_specs=[pl.BlockSpec(memory_space=pltpu.HBM)] * 6,
        out_specs=VMEM,
        scratch_shapes=[pltpu.SMEM(counts.shape, counts.dtype)]
        + [pltpu.VMEM(ref.shape, ref.dtype) for ref in (tokens, occupancy, grad, out, lse)]
        + [pltpu.SemaphoreType.DMA((6,))],
        compiler_params=params(60),
    )(counts, tokens, occupancy, grad, out, lse)
    got = swap(sent, "x")
    other = sibling(got)
    grads = pl.pallas_call(
        turn_kernel,
        out_shape=shape((2 * groups, rows * chips, width)),
        in_specs=[VMEM],
        out_specs=VMEM,
        compiler_params=params(8),
    )(got)
    grads = swap(grads, ("z", "c"))

    back = (chips, shard, width)
    each, half = width // groups, rows * heads // 2
    part = (groups, each + half, width)
    many = (2 * chips * shard, width)
    keep, give, parts = pl.pallas_call(
        main_kernel,
        out_shape=(shape(back), shape(back), shape(part)),
        in_specs=[SMEM] + [VMEM] * 6,
        out_specs=(VMEM,) * 3,
        scratch_shapes=[pltpu.VMEM((HEAD, latents), F32)] + [pltpu.VMEM(many, BF16)] * 2,
        compiler_params=params(40),
    )(head, got, other, grads, queries, w_key, w_value)
    kept, given = pl.pallas_call(
        share_kernel,
        out_shape=(shape(back, F32), shape(back)),
        in_specs=[SMEM] + [VMEM] * 4,
        out_specs=(VMEM,) * 2,
        compiler_params=params(16),
        cost_estimate=pl.CostEstimate(flops=270000000, bytes_accessed=3000000, transcendentals=0),
    )(head, keep, give, w_key, w_value)
    shares = pl.pallas_call(
        combine_kernel,
        out_shape=(shape((shard, width)),) * chips,
        in_specs=[SMEM] + [VMEM] * 2,
        out_specs=(VMEM,) * chips,
        compiler_params=params(16),
    )(chip, kept, sibling(given))
    own, *ahead = shares
    two = along_x(ahead[1], 2, chips)
    one = along_x(ahead[0], 1, chips)
    three = along_x(ahead[2], 3, chips)
    parts = swap(parts, "z")
    parts = pl.pallas_call(
        spread_kernel,
        out_shape=shape((windows, each + half, width)),
        in_specs=[VMEM],
        out_specs=VMEM,
        compiler_params=params(8),
    )(parts)
    parts = swap(parts, "y")
    weights, query_part = pl.pallas_call(
        total_kernel,
        out_shape=(shape((groups, each, width)), shape((2 * half, HEAD), F32)),
        in_specs=[VMEM],
        out_specs=(VMEM, VMEM),
        compiler_params=params(8),
    )(parts)
    weights, one, two = lax.optimization_barrier((weights, one, two))
    weights = swap(weights, "z").reshape(width, width)
    last = (chips, width + 2 * rows, width)
    sent = pl.pallas_call(
        gather_kernel,
        out_shape=shape(last),
        in_specs=[VMEM] * 2,
        out_specs=VMEM,
        compiler_params=params(16),
    )(weights, query_part)
    sent, *shares = lax.optimization_barrier((sent, own, one, two, three))
    got = swap(sent, "x")
    other = sibling(got)
    grad_tokens = pl.pallas_call(
        tokens_kernel,
        out_shape=shape((shard, width)),
        in_specs=[SMEM] + [VMEM] * (chips + 2),
        out_specs=VMEM,
        compiler_params=params(16),
        cost_estimate=pl.CostEstimate(flops=2000000, bytes_accessed=1000000, transcendentals=256),
    )(counts, *shares, tokens, occupancy)
    query_rows, key_total, value_total = pl.pallas_call(
        finish_kernel,
        out_shape=(
            shape((rows, heads * HEAD), F32),
            shape((width, heads * HEAD), F32),
            shape((width, heads * HEAD), F32),
        ),
        in_specs=[SMEM] + [VMEM] * 2,
        out_specs=(VMEM,) * 3,
        compiler_params=params(16),
    )(core, got, other)
    return grad_tokens[None], query_rows, key_total, value_total


def solution(mesh):
    seq, dp = mesh.shape["seq"], mesh.shape["dp"]
    split = Mesh(mesh.devices.reshape(seq // 8, 4, 2, dp), ("z", "x", "c", "y"))
    both = ("z", "x", "c")
    rows = P("y", both, None)
    return jax.shard_map(
        body,
        mesh=split,
        in_specs=(rows, P("y", both), P("y", both), P(), rows, rows, rows, P(), P()),
        out_specs=(rows, P(both, None), P(), P()),
        check_vma=False,
    )
```

```python
import math

import jax
import jax.numpy as jnp
from jax import lax
from jax.experimental import pallas as pl
from jax.experimental.pallas import tpu as pltpu
from jax.sharding import Mesh
from jax.sharding import PartitionSpec as P

HEAD = 128
ROWS = 8
BLOCK = 512
EPS = 1e-05
LOG2E = math.log2(math.e)
F32, BF16 = jnp.float32, jnp.bfloat16
VMEM = pl.BlockSpec(memory_space=pltpu.VMEM)
HBM = pl.BlockSpec(memory_space=pltpu.HBM)
SMEM = pl.BlockSpec(memory_space=pltpu.SMEM)


def params(mib):
    return pltpu.CompilerParams(vmem_limit_bytes=mib * 1024 * 1024)


def mm(left, right, left_dim, right_dim):
    return lax.dot_general(
        left, right, (((left_dim,), (right_dim,)), ((), ())), preferred_element_type=F32
    )


def layer_norm(tokens):
    center = tokens - jnp.mean(tokens, axis=-1, keepdims=True)
    inverse = lax.rsqrt(jnp.mean(center * center, axis=-1, keepdims=True) + EPS)
    return center * inverse, inverse


def live_rows(occupancy, count, width):
    shard = occupancy.shape[1]
    place = lax.broadcasted_iota(jnp.int32, (1, shard), 1)
    live = jnp.where(place < count, occupancy, 0).astype(F32)
    return jnp.broadcast_to(live, (width, shard)).T


def three_parts(column):
    parts = []
    for _ in range(3):
        part = column.astype(BF16).astype(F32)
        parts.append(part)
        column = column - part
    return parts


def columns_of(head):
    return pl.ds(pl.multiple_of(head[0] * HEAD, HEAD), HEAD)


def pack_kernel(*refs):
    sources, sent, held, (masked, extra_rows, taken, left) = refs[:6], refs[6], refs[7:13], refs[13:]
    copies = [
        pltpu.make_async_copy(source, target, taken.at[at])
        for at, (source, target) in enumerate(zip(sources, held))
    ]
    for copy in copies:
        copy.start()
    counts, tokens, occupancy, grad, out, lse = held
    chips, (shard, width) = sent.shape[0], tokens.shape
    for copy in copies[:3]:
        copy.wait()
    live = live_rows(occupancy[...], counts[0, 0], width)
    masked[...] = jnp.where(live > 0.0, tokens[...].astype(F32), 0.0).astype(BF16)
    leaving = [
        pltpu.make_async_copy(masked, sent.at[chip, pl.ds(0, shard)], left.at[0, chip])
        for chip in range(chips)
    ]
    for copy in leaving:
        copy.start()
    for copy in copies[3:]:
        copy.wait()
    rows = grad.shape[0]
    lane = lax.broadcasted_iota(jnp.int32, (rows, HEAD), 1)
    for chip in range(chips):
        extras, grads = [], []
        for head in (2 * chip, 2 * chip + 1):
            cols = slice(head * HEAD, (head + 1) * HEAD)
            grad_f32 = grad[:, cols].astype(F32)
            delta = jnp.sum(grad_f32 * out[:, cols].astype(F32), axis=1, keepdims=True)
            extra = jnp.zeros((rows, HEAD), F32)
            for at, part in enumerate(three_parts(lse[:, head : head + 1]) + three_parts(delta)):
                extra = jnp.where(lane == at, part, extra)
            extras.append(extra)
            grads.append(grad_f32)
        both = jnp.concatenate(
            [jnp.concatenate(grads, axis=1), jnp.concatenate(extras, axis=1)], axis=0
        )
        extra_rows[chip] = both.astype(BF16)
        copy = pltpu.make_async_copy(
            extra_rows.at[chip], sent.at[chip, pl.ds(shard, 2 * rows)], left.at[1, chip]
        )
        copy.start()
        leaving.append(copy)
    for copy in leaving:
        copy.wait()


def turn_kernel(got, sent):
    chips, width = got.shape[0], got.shape[2]
    shard = got.shape[1] - sent.shape[1] // chips * 2
    pieces = [got[chip, shard:, :].astype(F32) for chip in range(chips)]
    rows = sent.shape[1] // chips
    grads = jnp.concatenate([piece[:rows] for piece in pieces], axis=0)
    extras = jnp.concatenate([piece[rows:] for piece in pieces], axis=0)
    for core in range(2):
        cols = slice(core * HEAD, (core + 1) * HEAD)
        both = jnp.concatenate([grads[:, cols], extras[:, cols]], axis=1).astype(BF16)
        for group in range(sent.shape[0] // 2):
            sent[2 * group + core] = both


def latent_order(got, chips):
    rows = got.shape[1] // chips
    blocks = [got[at].astype(F32) for at in range(got.shape[0])]
    return jnp.concatenate(
        [
            blocks[2 * group + core][chip * rows : (chip + 1) * rows]
            for group in range(got.shape[0] // 2)
            for chip in range(chips)
            for core in range(2)
        ],
        axis=0,
    )


def share_kernel(head, keep, give, w_key, w_value, kept, given):
    cols = columns_of(head)
    weights = jnp.concatenate([w_key[:, cols], w_value[:, cols]], axis=1)
    for chip in range(keep.shape[0]):
        kept[chip] = mm(keep[chip], weights, 1, 1)
        given[chip] = mm(give[chip], weights, 1, 1).astype(BF16)


def main_kernel(
    head, mine, other, got, query, w_key, w_value, keep, give, parts, query_sum, normals, grads
):
    cols = columns_of(head)
    chips, shard = keep.shape[0], keep.shape[1]
    scale = 1.0 / math.sqrt(HEAD)
    rows = latent_order(got, chips)
    grad = rows[:, :HEAD].astype(BF16)
    extra = rows[:, HEAD:].T
    lse = (extra[0:1] + extra[1:2] + extra[2:3]) * LOG2E
    delta = extra[3:4] + extra[4:5] + extra[5:6]
    queries = query[:, cols]
    weights = jnp.concatenate([w_key[:, cols], w_value[:, cols]], axis=1)
    per = BLOCK // shard
    for block in range(2 * chips // per):
        first = block * per
        source, target = (mine, keep) if first < chips else (other, give)
        spots = [(first + at) % chips for at in range(per)]
        tokens = jnp.concatenate([source[spot, :shard, :] for spot in spots], axis=0)
        normal = layer_norm(tokens.astype(F32))[0].astype(BF16)
        both = jnp.dot(normal, weights, preferred_element_type=F32).astype(BF16)
        keys, values = both[:, :HEAD], both[:, HEAD:]
        probs = jnp.exp2(mm(keys, queries, 1, 1) * (scale * LOG2E) - lse)
        grad_values = jnp.dot(probs.astype(BF16), grad, preferred_element_type=F32)
        grad_probs = mm(values, grad, 1, 1)
        grad_scores = (scale * probs * (grad_probs - delta)).astype(BF16)
        grad_keys = jnp.dot(grad_scores, queries, preferred_element_type=F32)
        grad_both = jnp.concatenate([grad_keys, grad_values], axis=1).astype(BF16)
        for at, spot in enumerate(spots):
            target[spot] = grad_both[at * shard : (at + 1) * shard]
        query_part = mm(keys, grad_scores, 0, 0)
        if block == 0:
            query_sum[...] = query_part
        else:
            query_sum[...] += query_part
        normals[block * BLOCK : (block + 1) * BLOCK, :] = normal
        grads[block * BLOCK : (block + 1) * BLOCK, :] = grad_both
    turned = query_sum[...].T
    totals = mm(normals[...], grads[...], 0, 0)
    halves = parts.shape[0] // 2
    for at in range(parts.shape[0]):
        start = at % halves * ROWS
        cols = slice(at // halves * HEAD, (at // halves + 1) * HEAD)
        piece = [totals[start : start + ROWS, cols], turned[at * ROWS : (at + 1) * ROWS]]
        parts[at] = jnp.concatenate(piece, axis=1).astype(BF16)


def add_up(got):
    total = got[0].astype(F32)
    for at in range(1, got.shape[0]):
        total = total + got[at].astype(F32)
    return total


def spread_kernel(got, sent):
    total = add_up(got).astype(BF16)
    for at in range(sent.shape[0]):
        sent[at] = total


def combine_kernel(chip, kept, theirs, *shares):
    chips = kept.shape[0]
    for ahead in range(chips):
        at = lax.rem(chip[0] + ahead, chips)
        shares[ahead][...] = (kept[at] + theirs[at].astype(F32)).astype(BF16)


def gather_kernel(group, got, sent):
    chips = sent.shape[0]
    halves = got.shape[0] // 2
    depth = halves * ROWS
    pieces = [got[at].astype(F32)[:, :HEAD] for at in range(2 * halves)]
    weights = jnp.concatenate(
        [jnp.concatenate(pieces[:halves], axis=0), jnp.concatenate(pieces[halves:], axis=0)], axis=1
    ).astype(BF16)
    for chip in range(chips):
        sent[chip, :depth, :] = weights
        first = group[0] * 2 * chips + 2 * chip
        rows = [got[first + core].astype(F32) for core in range(2)]
        sent[chip, depth:, :] = jnp.concatenate(rows, axis=0).astype(BF16)


def place_totals(core, got, targets, staged, done):
    copies = []
    depth = staged.shape[2]
    for chip in range(staged.shape[0]):
        both = got[chip, :depth, :].astype(F32)
        cols = pl.ds(pl.multiple_of((2 * chip + core) * HEAD, HEAD), HEAD)
        for at, target in enumerate(targets):
            staged[chip, at] = both[:, at * HEAD : (at + 1) * HEAD]
            copy = pltpu.make_async_copy(
                staged.at[chip, at], target.at[:, cols], done.at[chip, at]
            )
            copy.start()
            copies.append(copy)
    return copies


def tokens_kernel(core, counts, got, *refs):
    shares, (tokens, occupancy, grad_tokens, key_total, value_total, staged, done) = (
        refs[:-7],
        refs[-7:],
    )
    copies = place_totals(core[0], got, (key_total, value_total), staged, done)
    width = tokens.shape[1]
    normal, inverse = layer_norm(tokens[...].astype(F32))
    grad_normal = shares[0][...].astype(F32)
    for share in shares[1:]:
        grad_normal += share[...].astype(F32)
    live = live_rows(occupancy[...], counts[0, 0], width)
    grad_normal = jnp.where(live > 0.0, grad_normal, 0.0)
    grad_input = inverse * (
        grad_normal
        - jnp.mean(grad_normal, axis=-1, keepdims=True)
        - normal * jnp.mean(grad_normal * normal, axis=-1, keepdims=True)
    )
    grad_tokens[...] = grad_input.astype(BF16)
    for copy in copies:
        copy.wait()


def finish_kernel(
    core, got, other, key_half, value_half, query_rows, key_total, value_total, staged, done
):
    del key_half, value_half
    copies = place_totals(1 - core[0], other, (key_total, value_total), staged, done)
    rows, depth = query_rows.shape[0], staged.shape[2]
    first = core[0] == 0
    for chip in range(got.shape[0]):
        mine, theirs = (ref[chip, depth:, HEAD:].astype(F32) for ref in (got, other))
        mine = jnp.where(first, mine[:rows], mine[rows:])
        theirs = jnp.where(first, theirs[:rows], theirs[rows:])
        start = 2 * chip * HEAD
        query_rows[:, start : start + HEAD] = jnp.where(first, mine, theirs)
        query_rows[:, start + HEAD : start + 2 * HEAD] = jnp.where(first, theirs, mine)
    for copy in copies:
        copy.wait()


def swap(array, axis):
    return lax.all_to_all(array, axis, 0, 0, tiled=True)


def shape(dims, dtype=BF16):
    return jax.ShapeDtypeStruct(dims, dtype)


def sibling(array):
    return lax.ppermute(array, "c", ((0, 1), (1, 0)))


def body(tokens, occupancy, counts, queries, saved_lse, grad_out, attn_out, w_key, w_value):
    tokens, grad, out, lse = tokens[0], grad_out[0], attn_out[0], saved_lse[0]
    shard, width = tokens.shape
    latents, rows = queries.shape[0], grad.shape[0]
    chips, groups, windows = lax.axis_size("x"), lax.axis_size("z"), lax.axis_size("y")
    heads = lse.shape[1]
    core, chip, group = (lax.axis_index(at).astype(jnp.int32) for at in ("c", "x", "z"))
    head = (2 * chip + core).reshape(1)
    core, chip, group = core.reshape(1), chip.reshape(1), group.reshape(1)
    tokens, head, core, chip, group = lax.optimization_barrier((tokens, head, core, chip, group))
    sent = pl.pallas_call(
        pack_kernel,
        out_shape=pltpu.HBM((chips, shard + 2 * rows, width), BF16),
        in_specs=[HBM] * 6,
        out_specs=HBM,
        scratch_shapes=[pltpu.SMEM(counts.shape, counts.dtype)]
        + [pltpu.VMEM(ref.shape, ref.dtype) for ref in (tokens, occupancy, grad, out, lse)]
        + [pltpu.VMEM((shard, width), BF16), pltpu.VMEM((chips, 2 * rows, width), BF16)]
        + [pltpu.SemaphoreType.DMA((6,)), pltpu.SemaphoreType.DMA((2, chips))],
        compiler_params=params(60),
    )(counts, tokens, occupancy, grad, out, lse)
    got = swap(sent, "x")
    other = sibling(got)
    grads = pl.pallas_call(
        turn_kernel,
        out_shape=shape((2 * groups, rows * chips, width)),
        in_specs=[VMEM],
        out_specs=VMEM,
        compiler_params=params(8),
    )(got)
    grads = swap(grads, ("z", "c"))

    back = (chips, shard, width)
    part = (groups * windows, ROWS, width)
    many = (2 * chips * shard, width)
    keep, give, parts = pl.pallas_call(
        main_kernel,
        out_shape=(shape(back), shape(back), shape(part)),
        in_specs=[SMEM] + [VMEM] * 6,
        out_specs=(VMEM,) * 3,
        scratch_shapes=[pltpu.VMEM((HEAD, latents), F32)] + [pltpu.VMEM(many, BF16)] * 2,
        compiler_params=params(40),
    )(head, got, other, grads, queries, w_key, w_value)
    kept, given = pl.pallas_call(
        share_kernel,
        out_shape=(shape(back, F32), shape(back)),
        in_specs=[SMEM] + [VMEM] * 4,
        out_specs=(VMEM,) * 2,
        compiler_params=params(16),
        cost_estimate=pl.CostEstimate(flops=270000000, bytes_accessed=3000000, transcendentals=0),
    )(head, keep, give, w_key, w_value)
    shares = pl.pallas_call(
        combine_kernel,
        out_shape=(shape((shard, width)),) * chips,
        in_specs=[SMEM] + [VMEM] * 2,
        out_specs=(VMEM,) * chips,
        compiler_params=params(16),
    )(chip, kept, sibling(given))
    shares = [shares[0]] + [
        lax.ppermute(share, "x", [(at, (at + ahead) % chips) for at in range(chips)])
        for ahead, share in enumerate(shares[1:], 1)
    ]
    parts = swap(parts, ("z", "y"))
    parts = pl.pallas_call(
        spread_kernel,
        out_shape=shape(part),
        in_specs=[VMEM],
        out_specs=VMEM,
        compiler_params=params(8),
    )(parts)
    parts = swap(parts, ("z", "y"))
    last = (chips, width + 2 * rows, width)
    sent = pl.pallas_call(
        gather_kernel,
        out_shape=shape(last),
        in_specs=[SMEM, VMEM],
        out_specs=VMEM,
        compiler_params=params(16),
    )(group, parts)
    sent, *shares = lax.optimization_barrier((sent, *shares))
    got = swap(sent, "x")
    other = sibling(got)
    total = pltpu.HBM((width, heads * HEAD), F32)
    staging = [
        pltpu.VMEM((chips, 2, width, HEAD), F32),
        pltpu.SemaphoreType.DMA((chips, 2)),
    ]
    grad_tokens, key_total, value_total = pl.pallas_call(
        tokens_kernel,
        out_shape=(shape((shard, width)), total, total),
        in_specs=[SMEM] * 2 + [VMEM] * (chips + 3),
        out_specs=(VMEM, HBM, HBM),
        scratch_shapes=staging,
        compiler_params=params(16),
        cost_estimate=pl.CostEstimate(flops=2000000, bytes_accessed=3000000, transcendentals=256),
    )(core, counts, got, *shares, tokens, occupancy)
    query_rows, key_total, value_total = pl.pallas_call(
        finish_kernel,
        out_shape=(shape((rows, heads * HEAD), F32), total, total),
        in_specs=[SMEM] + [VMEM] * 2 + [HBM] * 2,
        out_specs=(VMEM, HBM, HBM),
        input_output_aliases={3: 1, 4: 2},
        scratch_shapes=staging,
        compiler_params=params(16),
    )(core, got, other, key_total, value_total)
    return grad_tokens[None], query_rows, key_total, value_total


def solution(mesh):
    seq, dp = mesh.shape["seq"], mesh.shape["dp"]
    split = Mesh(mesh.devices.reshape(seq // 8, 4, 2, dp), ("z", "x", "c", "y"))
    both = ("z", "x", "c")
    rows = P("y", both, None)
    return jax.shard_map(
        body,
        mesh=split,
        in_specs=(rows, P("y", both), P("y", both), P(), rows, rows, rows, P(), P()),
        out_specs=(rows, P(both, None), P(), P()),
        check_vma=False,
    )
```

```python
import math

import jax
import jax.numpy as jnp
from jax import lax
from jax.experimental import pallas as pl
from jax.experimental.pallas import tpu as pltpu
from jax.sharding import Mesh
from jax.sharding import PartitionSpec as P

HEAD = 128
ROWS = 8
BLOCK = 512
EPS = 1e-05
LOG2E = math.log2(math.e)
F32, BF16 = jnp.float32, jnp.bfloat16
VMEM = pl.BlockSpec(memory_space=pltpu.VMEM)
HBM = pl.BlockSpec(memory_space=pltpu.HBM)
SMEM = pl.BlockSpec(memory_space=pltpu.SMEM)


def params(mib):
    return pltpu.CompilerParams(vmem_limit_bytes=mib * 1024 * 1024)


def mm(left, right, left_dim, right_dim):
    return lax.dot_general(
        left, right, (((left_dim,), (right_dim,)), ((), ())), preferred_element_type=F32
    )


def layer_norm(tokens):
    center = tokens - jnp.mean(tokens, axis=-1, keepdims=True)
    inverse = lax.rsqrt(jnp.mean(center * center, axis=-1, keepdims=True) + EPS)
    return center * inverse, inverse


def live_rows(occupancy, count, width):
    shard = occupancy.shape[1]
    place = lax.broadcasted_iota(jnp.int32, (1, shard), 1)
    live = jnp.where(place < count, occupancy, 0).astype(F32)
    return jnp.broadcast_to(live, (width, shard)).T


def three_parts(column):
    parts = []
    for _ in range(3):
        part = column.astype(BF16).astype(F32)
        parts.append(part)
        column = column - part
    return parts


def columns_of(head):
    return pl.ds(pl.multiple_of(head[0] * HEAD, HEAD), HEAD)


def pack_kernel(*refs):
    sources, sent, held, (masked, extra_rows, taken, left) = refs[:6], refs[6], refs[7:13], refs[13:]
    copies = [
        pltpu.make_async_copy(source, target, taken.at[at])
        for at, (source, target) in enumerate(zip(sources, held))
    ]
    for copy in copies:
        copy.start()
    counts, tokens, occupancy, grad, out, lse = held
    chips, (shard, width) = sent.shape[0], tokens.shape
    for copy in copies[:3]:
        copy.wait()
    live = live_rows(occupancy[...], counts[0, 0], width)
    masked[...] = jnp.where(live > 0.0, tokens[...].astype(F32), 0.0).astype(BF16)
    leaving = [
        pltpu.make_async_copy(masked, sent.at[chip, pl.ds(0, shard)], left.at[0, chip])
        for chip in range(chips)
    ]
    for copy in leaving:
        copy.start()
    for copy in copies[3:]:
        copy.wait()
    rows = grad.shape[0]
    lane = lax.broadcasted_iota(jnp.int32, (rows, HEAD), 1)
    for chip in range(chips):
        extras, grads = [], []
        for head in (2 * chip, 2 * chip + 1):
            cols = slice(head * HEAD, (head + 1) * HEAD)
            grad_f32 = grad[:, cols].astype(F32)
            delta = jnp.sum(grad_f32 * out[:, cols].astype(F32), axis=1, keepdims=True)
            extra = jnp.zeros((rows, HEAD), F32)
            for at, part in enumerate(three_parts(lse[:, head : head + 1]) + three_parts(delta)):
                extra = jnp.where(lane == at, part, extra)
            extras.append(extra)
            grads.append(grad_f32)
        both = jnp.concatenate(
            [jnp.concatenate(grads, axis=1), jnp.concatenate(extras, axis=1)], axis=0
        )
        extra_rows[chip] = both.astype(BF16)
        copy = pltpu.make_async_copy(
            extra_rows.at[chip], sent.at[chip, pl.ds(shard, 2 * rows)], left.at[1, chip]
        )
        copy.start()
        leaving.append(copy)
    for copy in leaving:
        copy.wait()


def turn_kernel(spot, got, sent):
    chips = got.shape[0]
    shard = got.shape[1] - 2 * ROWS
    pieces = [got[chip, shard:, :].astype(F32) for chip in range(chips)]
    blank = jnp.zeros((ROWS, HEAD), F32)
    for core in range(2):
        cols = slice(core * HEAD, (core + 1) * HEAD)
        early, late = [], []
        for piece in pieces:
            early += [piece[ROWS:, cols], blank]
            late += [blank, piece[ROWS:, cols]]
        early, late = jnp.concatenate(early, axis=0), jnp.concatenate(late, axis=0)
        placed = jnp.where(spot[1] == 0, early, late)
        empty = jnp.zeros_like(placed)
        placed = jnp.concatenate(
            [jnp.where(spot[0] == 0, placed, empty), jnp.where(spot[0] == 0, empty, placed)], axis=0
        )
        both = [piece[:ROWS, cols] for piece in pieces] + [placed.T[:ROWS]]
        both = jnp.concatenate(both, axis=0).astype(BF16)
        for group in range(sent.shape[0] // 2):
            sent[2 * group + core] = both


def latent_order(got, chips):
    blocks = [got[at].astype(F32) for at in range(got.shape[0])]
    rows = [
        blocks[2 * group + core][chip * ROWS : (chip + 1) * ROWS]
        for group in range(got.shape[0] // 2)
        for chip in range(chips)
        for core in range(2)
    ]
    tails = [block[chips * ROWS :] for block in blocks]
    lines = jnp.concatenate(
        [
            tails[at] + tails[at + 1] + tails[at + 2] + tails[at + 3]
            for at in range(0, len(tails), 4)
        ],
        axis=1,
    )
    lse = (lines[0:1] + lines[1:2] + lines[2:3]) * LOG2E
    delta = lines[3:4] + lines[4:5] + lines[5:6]
    return jnp.concatenate(rows, axis=0).astype(BF16), lse, delta


def share_kernel(head, keep, give, w_key, w_value, kept, given):
    cols = columns_of(head)
    weights = jnp.concatenate([w_key[:, cols], w_value[:, cols]], axis=1)
    for chip in range(keep.shape[0]):
        kept[chip] = mm(keep[chip], weights, 1, 1)
        given[chip] = mm(give[chip], weights, 1, 1).astype(BF16)


def main_kernel(
    head, mine, other, got, query, w_key, w_value, keep, give, parts, query_sum, normals, grads
):
    cols = columns_of(head)
    chips, shard = keep.shape[0], keep.shape[1]
    scale = 1.0 / math.sqrt(HEAD)
    grad, lse, delta = latent_order(got, chips)
    queries = query[:, cols]
    weights = jnp.concatenate([w_key[:, cols], w_value[:, cols]], axis=1)
    per = BLOCK // shard
    for block in range(2 * chips // per):
        first = block * per
        source, target = (mine, keep) if first < chips else (other, give)
        spots = [(first + at) % chips for at in range(per)]
        tokens = jnp.concatenate([source[spot, :shard, :] for spot in spots], axis=0)
        normal = layer_norm(tokens.astype(F32))[0].astype(BF16)
        both = jnp.dot(normal, weights, preferred_element_type=F32).astype(BF16)
        keys, values = both[:, :HEAD], both[:, HEAD:]
        probs = jnp.exp2(mm(keys, queries, 1, 1) * (scale * LOG2E) - lse)
        grad_values = jnp.dot(probs.astype(BF16), grad, preferred_element_type=F32)
        grad_probs = mm(values, grad, 1, 1)
        grad_scores = (scale * probs * (grad_probs - delta)).astype(BF16)
        grad_keys = jnp.dot(grad_scores, queries, preferred_element_type=F32)
        grad_both = jnp.concatenate([grad_keys, grad_values], axis=1).astype(BF16)
        for at, spot in enumerate(spots):
            target[spot] = grad_both[at * shard : (at + 1) * shard]
        query_part = mm(keys, grad_scores, 0, 0)
        if block == 0:
            query_sum[...] = query_part
        else:
            query_sum[...] += query_part
        normals[block * BLOCK : (block + 1) * BLOCK, :] = normal
        grads[block * BLOCK : (block + 1) * BLOCK, :] = grad_both
    turned = query_sum[...].T
    totals = mm(normals[...], grads[...], 0, 0)
    halves = parts.shape[0] // 2
    for at in range(parts.shape[0]):
        start = at % halves * ROWS
        cols = slice(at // halves * HEAD, (at // halves + 1) * HEAD)
        piece = [totals[start : start + ROWS, cols], turned[at * ROWS : (at + 1) * ROWS]]
        parts[at] = jnp.concatenate(piece, axis=1).astype(BF16)


def add_up(got):
    total = got[0].astype(F32)
    for at in range(1, got.shape[0]):
        total = total + got[at].astype(F32)
    return total


def spread_kernel(got, sent):
    total = add_up(got).astype(BF16)
    for at in range(sent.shape[0]):
        sent[at] = total


def combine_kernel(chip, kept, theirs, *shares):
    chips = kept.shape[0]
    for ahead in range(chips):
        at = lax.rem(chip[0] + ahead, chips)
        shares[ahead][...] = (kept[at] + theirs[at].astype(F32)).astype(BF16)


def gather_kernel(group, got, sent):
    chips = sent.shape[0]
    halves = got.shape[0] // 2
    depth = halves * ROWS
    pieces = [got[at].astype(F32)[:, :HEAD] for at in range(2 * halves)]
    weights = jnp.concatenate(
        [jnp.concatenate(pieces[:halves], axis=0), jnp.concatenate(pieces[halves:], axis=0)], axis=1
    ).astype(BF16)
    for chip in range(chips):
        sent[chip, :depth, :] = weights
        first = group[0] * 2 * chips + 2 * chip
        rows = [got[first + core].astype(F32) for core in range(2)]
        sent[chip, depth:, :] = jnp.concatenate(rows, axis=0).astype(BF16)


def place_totals(core, got, targets, staged, done):
    copies = []
    depth = staged.shape[2]
    for chip in range(staged.shape[0]):
        both = got[chip, :depth, :].astype(F32)
        cols = pl.ds(pl.multiple_of((2 * chip + core) * HEAD, HEAD), HEAD)
        for at, target in enumerate(targets):
            staged[chip, at] = both[:, at * HEAD : (at + 1) * HEAD]
            copy = pltpu.make_async_copy(
                staged.at[chip, at], target.at[:, cols], done.at[chip, at]
            )
            copy.start()
            copies.append(copy)
    return copies


def tokens_kernel(core, counts, got, *refs):
    shares, (tokens, occupancy, grad_tokens, key_total, value_total, staged, done) = (
        refs[:-7],
        refs[-7:],
    )
    copies = place_totals(core[0], got, (key_total, value_total), staged, done)
    width = tokens.shape[1]
    normal, inverse = layer_norm(tokens[...].astype(F32))
    grad_normal = shares[0][...].astype(F32)
    for share in shares[1:]:
        grad_normal += share[...].astype(F32)
    live = live_rows(occupancy[...], counts[0, 0], width)
    grad_normal = jnp.where(live > 0.0, grad_normal, 0.0)
    grad_input = inverse * (
        grad_normal
        - jnp.mean(grad_normal, axis=-1, keepdims=True)
        - normal * jnp.mean(grad_normal * normal, axis=-1, keepdims=True)
    )
    grad_tokens[...] = grad_input.astype(BF16)
    for copy in copies:
        copy.wait()


def finish_kernel(
    core, got, other, key_half, value_half, query_rows, key_total, value_total, staged, done
):
    del key_half, value_half
    copies = place_totals(1 - core[0], other, (key_total, value_total), staged, done)
    rows, depth = query_rows.shape[0], staged.shape[2]
    first = core[0] == 0
    for chip in range(got.shape[0]):
        mine, theirs = (ref[chip, depth:, HEAD:].astype(F32) for ref in (got, other))
        mine = jnp.where(first, mine[:rows], mine[rows:])
        theirs = jnp.where(first, theirs[:rows], theirs[rows:])
        start = 2 * chip * HEAD
        query_rows[:, start : start + HEAD] = jnp.where(first, mine, theirs)
        query_rows[:, start + HEAD : start + 2 * HEAD] = jnp.where(first, theirs, mine)
    for copy in copies:
        copy.wait()


def swap(array, axis):
    return lax.all_to_all(array, axis, 0, 0, tiled=True)


def shape(dims, dtype=BF16):
    return jax.ShapeDtypeStruct(dims, dtype)


def sibling(array):
    return lax.ppermute(array, "c", ((0, 1), (1, 0)))


def body(tokens, occupancy, counts, queries, saved_lse, grad_out, attn_out, w_key, w_value):
    tokens, grad, out, lse = tokens[0], grad_out[0], attn_out[0], saved_lse[0]
    shard, width = tokens.shape
    latents, rows = queries.shape[0], grad.shape[0]
    chips, groups, windows = lax.axis_size("x"), lax.axis_size("z"), lax.axis_size("y")
    heads = lse.shape[1]
    core, chip, group = (lax.axis_index(at).astype(jnp.int32) for at in ("c", "x", "z"))
    head = (2 * chip + core).reshape(1)
    spot = jnp.stack([lax.rem(group, 2), core])
    core, chip, group = core.reshape(1), chip.reshape(1), group.reshape(1)
    tokens, head, core, chip, group, spot = lax.optimization_barrier(
        (tokens, head, core, chip, group, spot)
    )
    sent = pl.pallas_call(
        pack_kernel,
        out_shape=pltpu.HBM((chips, shard + 2 * rows, width), BF16),
        in_specs=[HBM] * 6,
        out_specs=HBM,
        scratch_shapes=[pltpu.SMEM(counts.shape, counts.dtype)]
        + [pltpu.VMEM(ref.shape, ref.dtype) for ref in (tokens, occupancy, grad, out, lse)]
        + [pltpu.VMEM((shard, width), BF16), pltpu.VMEM((chips, 2 * rows, width), BF16)]
        + [pltpu.SemaphoreType.DMA((6,)), pltpu.SemaphoreType.DMA((2, chips))],
        compiler_params=params(60),
    )(counts, tokens, occupancy, grad, out, lse)
    got = swap(sent, "x")
    other = sibling(got)
    grads = pl.pallas_call(
        turn_kernel,
        out_shape=shape((2 * groups, (chips + 1) * rows, HEAD)),
        in_specs=[SMEM, VMEM],
        out_specs=VMEM,
        compiler_params=params(8),
    )(spot, got)
    grads = swap(grads, ("z", "c"))

    back = (chips, shard, width)
    part = (groups * windows, ROWS, width)
    many = (2 * chips * shard, width)
    keep, give, parts = pl.pallas_call(
        main_kernel,
        out_shape=(shape(back), shape(back), shape(part)),
        in_specs=[SMEM] + [VMEM] * 6,
        out_specs=(VMEM,) * 3,
        scratch_shapes=[pltpu.VMEM((HEAD, latents), F32)] + [pltpu.VMEM(many, BF16)] * 2,
        compiler_params=params(40),
    )(head, got, other, grads, queries, w_key, w_value)
    kept, given = pl.pallas_call(
        share_kernel,
        out_shape=(shape(back, F32), shape(back)),
        in_specs=[SMEM] + [VMEM] * 4,
        out_specs=(VMEM,) * 2,
        compiler_params=params(16),
        cost_estimate=pl.CostEstimate(flops=270000000, bytes_accessed=3000000, transcendentals=0),
    )(head, keep, give, w_key, w_value)
    shares = pl.pallas_call(
        combine_kernel,
        out_shape=(shape((shard, width)),) * chips,
        in_specs=[SMEM] + [VMEM] * 2,
        out_specs=(VMEM,) * chips,
        compiler_params=params(16),
    )(chip, kept, sibling(given))
    shares = [shares[0]] + [
        lax.ppermute(shares[ahead], "x", [(at, (at + ahead) % chips) for at in range(chips)])
        for ahead in (2, 1, 3)
    ]
    parts = swap(parts, ("z", "y"))
    parts = pl.pallas_call(
        spread_kernel,
        out_shape=shape(part),
        in_specs=[VMEM],
        out_specs=VMEM,
        compiler_params=params(8),
    )(parts)
    parts = swap(parts, ("z", "y"))
    last = (chips, width + 2 * rows, width)
    sent = pl.pallas_call(
        gather_kernel,
        out_shape=shape(last),
        in_specs=[SMEM, VMEM],
        out_specs=VMEM,
        compiler_params=params(16),
    )(group, parts)
    sent, *shares = lax.optimization_barrier((sent, *shares))
    got = swap(sent, "x")
    other = sibling(got)
    total = pltpu.HBM((width, heads * HEAD), F32)
    staging = [
        pltpu.VMEM((chips, 2, width, HEAD), F32),
        pltpu.SemaphoreType.DMA((chips, 2)),
    ]
    grad_tokens, key_total, value_total = pl.pallas_call(
        tokens_kernel,
        out_shape=(shape((shard, width)), total, total),
        in_specs=[SMEM] * 2 + [VMEM] * (chips + 3),
        out_specs=(VMEM, HBM, HBM),
        scratch_shapes=staging,
        compiler_params=params(16),
        cost_estimate=pl.CostEstimate(flops=2000000, bytes_accessed=3000000, transcendentals=256),
    )(core, counts, got, *shares, tokens, occupancy)
    query_rows, key_total, value_total = pl.pallas_call(
        finish_kernel,
        out_shape=(shape((rows, heads * HEAD), F32), total, total),
        in_specs=[SMEM] + [VMEM] * 2 + [HBM] * 2,
        out_specs=(VMEM, HBM, HBM),
        input_output_aliases={3: 1, 4: 2},
        scratch_shapes=staging,
        compiler_params=params(16),
    )(core, got, other, key_total, value_total)
    return grad_tokens[None], query_rows, key_total, value_total


def solution(mesh):
    seq, dp = mesh.shape["seq"], mesh.shape["dp"]
    split = Mesh(mesh.devices.reshape(seq // 8, 4, 2, dp), ("z", "x", "c", "y"))
    both = ("z", "x", "c")
    rows = P("y", both, None)
    return jax.shard_map(
        body,
        mesh=split,
        in_specs=(rows, P("y", both), P("y", both), P(), rows, rows, rows, P(), P()),
        out_specs=(rows, P(both, None), P(), P()),
        check_vma=False,
    )
```

```python
import math

import jax
import jax.numpy as jnp
from jax import lax
from jax.experimental import pallas as pl
from jax.experimental.pallas import tpu as pltpu
from jax.sharding import Mesh
from jax.sharding import PartitionSpec as P

HEAD = 128
ROWS = 8
BLOCK = 512
EPS = 1e-05
LOG2E = math.log2(math.e)
F32, BF16 = jnp.float32, jnp.bfloat16
VMEM = pl.BlockSpec(memory_space=pltpu.VMEM)
HBM = pl.BlockSpec(memory_space=pltpu.HBM)
SMEM = pl.BlockSpec(memory_space=pltpu.SMEM)


def params(mib):
    return pltpu.CompilerParams(vmem_limit_bytes=mib * 1024 * 1024)


def mm(left, right, left_dim, right_dim):
    return lax.dot_general(
        left, right, (((left_dim,), (right_dim,)), ((), ())), preferred_element_type=F32
    )


def layer_norm(tokens):
    center = tokens - jnp.mean(tokens, axis=-1, keepdims=True)
    inverse = lax.rsqrt(jnp.mean(center * center, axis=-1, keepdims=True) + EPS)
    return center * inverse, inverse


def live_rows(occupancy, count, width):
    shard = occupancy.shape[1]
    place = lax.broadcasted_iota(jnp.int32, (1, shard), 1)
    live = jnp.where(place < count, occupancy, 0).astype(F32)
    return jnp.broadcast_to(live, (width, shard)).T


def three_parts(column):
    parts = []
    for _ in range(3):
        part = column.astype(BF16).astype(F32)
        parts.append(part)
        column = column - part
    return parts


def columns_of(head):
    return pl.ds(pl.multiple_of(head[0] * HEAD, HEAD), HEAD)


def pack_kernel(*refs):
    sources, sent, held, (masked, extra_rows, taken, left) = refs[:6], refs[6], refs[7:13], refs[13:]
    copies = [
        pltpu.make_async_copy(source, target, taken.at[at])
        for at, (source, target) in enumerate(zip(sources, held))
    ]
    for copy in copies:
        copy.start()
    counts, tokens, occupancy, grad, out, lse = held
    chips, (shard, width) = sent.shape[0], tokens.shape
    for copy in copies[:3]:
        copy.wait()
    live = live_rows(occupancy[...], counts[0, 0], width)
    masked[...] = jnp.where(live > 0.0, tokens[...].astype(F32), 0.0).astype(BF16)
    leaving = [
        pltpu.make_async_copy(masked, sent.at[chip, pl.ds(0, shard)], left.at[0, chip])
        for chip in range(chips)
    ]
    for copy in leaving:
        copy.start()
    for copy in copies[3:]:
        copy.wait()
    rows = grad.shape[0]
    lane = lax.broadcasted_iota(jnp.int32, (rows, HEAD), 1)
    for chip in range(chips):
        extras, grads = [], []
        for head in (2 * chip, 2 * chip + 1):
            cols = slice(head * HEAD, (head + 1) * HEAD)
            grad_f32 = grad[:, cols].astype(F32)
            delta = jnp.sum(grad_f32 * out[:, cols].astype(F32), axis=1, keepdims=True)
            extra = jnp.zeros((rows, HEAD), F32)
            for at, part in enumerate(three_parts(lse[:, head : head + 1]) + three_parts(delta)):
                extra = jnp.where(lane == at + head % 2 * ROWS, part, extra)
            extras.append(extra)
            grads.append(grad_f32)
        both = jnp.concatenate(
            [jnp.concatenate(grads, axis=1), jnp.concatenate(extras, axis=1)], axis=0
        )
        extra_rows[chip] = both.astype(BF16)
        copy = pltpu.make_async_copy(
            extra_rows.at[chip], sent.at[chip, pl.ds(shard, 2 * rows)], left.at[1, chip]
        )
        copy.start()
        leaving.append(copy)
    for copy in leaving:
        copy.wait()


def turn_kernel(spot, got, sent):
    chips = got.shape[0]
    shard = got.shape[1] - 2 * ROWS
    pieces = [got[chip, shard:, :].astype(F32) for chip in range(chips)]
    blank = jnp.zeros((ROWS, HEAD), F32)
    early, late = [], []
    for piece in pieces:
        tail = piece[ROWS:, :HEAD] + piece[ROWS:, HEAD:]
        early += [tail, blank]
        late += [blank, tail]
    early, late = jnp.concatenate(early, axis=0), jnp.concatenate(late, axis=0)
    placed = jnp.where(spot[1] == 0, early, late)
    empty = jnp.zeros_like(placed)
    lines = jnp.concatenate(
        [jnp.where(spot[0] == 0, placed, empty), jnp.where(spot[0] == 0, empty, placed)], axis=0
    ).T
    for core in range(2):
        cols = slice(core * HEAD, (core + 1) * HEAD)
        both = [piece[:ROWS, cols] for piece in pieces]
        both = jnp.concatenate(both + [lines[core * ROWS : (core + 1) * ROWS]], axis=0).astype(BF16)
        for group in range(sent.shape[0] // 2):
            sent[2 * group + core] = both


def latent_order(got, chips):
    blocks = [got[at].astype(F32) for at in range(got.shape[0])]
    rows = [
        blocks[2 * group + core][chip * ROWS : (chip + 1) * ROWS]
        for group in range(got.shape[0] // 2)
        for chip in range(chips)
        for core in range(2)
    ]
    tails = [block[chips * ROWS :] for block in blocks]
    lines = jnp.concatenate(
        [
            tails[at] + tails[at + 1] + tails[at + 2] + tails[at + 3]
            for at in range(0, len(tails), 4)
        ],
        axis=1,
    )
    lse = (lines[0:1] + lines[1:2] + lines[2:3]) * LOG2E
    delta = lines[3:4] + lines[4:5] + lines[5:6]
    return jnp.concatenate(rows, axis=0).astype(BF16), lse, delta


def share_kernel(head, keep, give, w_key, w_value, kept, given):
    cols = columns_of(head)
    weights = jnp.concatenate([w_key[:, cols], w_value[:, cols]], axis=1)
    for chip in range(keep.shape[0]):
        kept[chip] = mm(keep[chip], weights, 1, 1)
        given[chip] = mm(give[chip], weights, 1, 1).astype(BF16)


def main_kernel(
    head, mine, other, got, query, w_key, w_value, keep, give, parts, query_sum, normals, grads
):
    cols = columns_of(head)
    chips, shard = keep.shape[0], keep.shape[1]
    scale = 1.0 / math.sqrt(HEAD)
    grad, lse, delta = latent_order(got, chips)
    queries = query[:, cols]
    weights = jnp.concatenate([w_key[:, cols], w_value[:, cols]], axis=1)
    per = BLOCK // shard
    for block in range(2 * chips // per):
        first = block * per
        source, target = (mine, keep) if first < chips else (other, give)
        spots = [(first + at) % chips for at in range(per)]
        tokens = jnp.concatenate([source[spot, :shard, :] for spot in spots], axis=0)
        normal = layer_norm(tokens.astype(F32))[0].astype(BF16)
        both = jnp.dot(normal, weights, preferred_element_type=F32).astype(BF16)
        keys, values = both[:, :HEAD], both[:, HEAD:]
        probs = jnp.exp2(mm(keys, queries, 1, 1) * (scale * LOG2E) - lse)
        grad_values = jnp.dot(probs.astype(BF16), grad, preferred_element_type=F32)
        grad_probs = mm(values, grad, 1, 1)
        grad_scores = (scale * probs * (grad_probs - delta)).astype(BF16)
        grad_keys = jnp.dot(grad_scores, queries, preferred_element_type=F32)
        grad_both = jnp.concatenate([grad_keys, grad_values], axis=1).astype(BF16)
        for at, spot in enumerate(spots):
            target[spot] = grad_both[at * shard : (at + 1) * shard]
        query_part = mm(keys, grad_scores, 0, 0)
        if block == 0:
            query_sum[...] = query_part
        else:
            query_sum[...] += query_part
        normals[block * BLOCK : (block + 1) * BLOCK, :] = normal
        grads[block * BLOCK : (block + 1) * BLOCK, :] = grad_both
    turned = query_sum[...].T
    totals = mm(normals[...], grads[...], 0, 0)
    halves = parts.shape[0] // 2
    for at in range(parts.shape[0]):
        start = at % halves * ROWS
        cols = slice(at // halves * HEAD, (at // halves + 1) * HEAD)
        query_at = (at % 8 * 8 + at // 8) * ROWS
        piece = [totals[start : start + ROWS, cols], turned[query_at : query_at + ROWS]]
        parts[at] = jnp.concatenate(piece, axis=1).astype(BF16)


def add_up(got):
    total = got[0].astype(F32)
    for at in range(1, got.shape[0]):
        total = total + got[at].astype(F32)
    return total


def spread_kernel(got, sent):
    total = add_up(got).astype(BF16)
    for at in range(sent.shape[0]):
        sent[at] = total


def combine_kernel(chip, kept, theirs, *shares):
    chips = kept.shape[0]
    for ahead in range(chips):
        at = lax.rem(chip[0] + ahead, chips)
        shares[ahead][...] = (kept[at] + theirs[at].astype(F32)).astype(BF16)


def gather_kernel(group, got, sent):
    chips = sent.shape[0]
    halves = got.shape[0] // 2
    depth = halves * ROWS
    pieces = [got[at].astype(F32)[:, :HEAD] for at in range(2 * halves)]
    weights = jnp.concatenate(
        [jnp.concatenate(pieces[:halves], axis=0), jnp.concatenate(pieces[halves:], axis=0)], axis=1
    ).astype(BF16)
    for chip in range(chips):
        sent[chip, :depth, :] = weights
        rows = [
            got[(2 * chip + core) * 2 * chips + group[0]].astype(F32) for core in range(2)
        ]
        sent[chip, depth:, :] = jnp.concatenate(rows, axis=0).astype(BF16)


def place_totals(core, got, targets, staged, done):
    copies = []
    depth = staged.shape[2]
    for chip in range(staged.shape[0]):
        both = got[chip, :depth, :].astype(F32)
        cols = pl.ds(pl.multiple_of((2 * chip + core) * HEAD, HEAD), HEAD)
        for at, target in enumerate(targets):
            staged[chip, at] = both[:, at * HEAD : (at + 1) * HEAD]
            copy = pltpu.make_async_copy(
                staged.at[chip, at], target.at[:, cols], done.at[chip, at]
            )
            copy.start()
            copies.append(copy)
    return copies


def tokens_kernel(core, counts, got, *refs):
    shares, (tokens, occupancy, grad_tokens, key_total, value_total, staged, done) = (
        refs[:-7],
        refs[-7:],
    )
    copies = place_totals(core[0], got, (key_total, value_total), staged, done)
    width = tokens.shape[1]
    normal, inverse = layer_norm(tokens[...].astype(F32))
    grad_normal = shares[0][...].astype(F32)
    for share in shares[1:]:
        grad_normal += share[...].astype(F32)
    live = live_rows(occupancy[...], counts[0, 0], width)
    grad_normal = jnp.where(live > 0.0, grad_normal, 0.0)
    grad_input = inverse * (
        grad_normal
        - jnp.mean(grad_normal, axis=-1, keepdims=True)
        - normal * jnp.mean(grad_normal * normal, axis=-1, keepdims=True)
    )
    grad_tokens[...] = grad_input.astype(BF16)
    for copy in copies:
        copy.wait()


def finish_kernel(
    core, got, other, key_half, value_half, query_rows, key_total, value_total, staged, done
):
    del key_half, value_half
    copies = place_totals(1 - core[0], other, (key_total, value_total), staged, done)
    rows, depth = query_rows.shape[0], staged.shape[2]
    first = core[0] == 0
    for chip in range(got.shape[0]):
        mine, theirs = (ref[chip, depth:, HEAD:].astype(F32) for ref in (got, other))
        mine = jnp.where(first, mine[:rows], mine[rows:])
        theirs = jnp.where(first, theirs[:rows], theirs[rows:])
        start = 2 * chip * HEAD
        query_rows[:, start : start + HEAD] = jnp.where(first, mine, theirs)
        query_rows[:, start + HEAD : start + 2 * HEAD] = jnp.where(first, theirs, mine)
    for copy in copies:
        copy.wait()


def swap(array, axis):
    return lax.all_to_all(array, axis, 0, 0, tiled=True)


def shape(dims, dtype=BF16):
    return jax.ShapeDtypeStruct(dims, dtype)


def sibling(array):
    return lax.ppermute(array, "c", ((0, 1), (1, 0)))


def body(tokens, occupancy, counts, queries, saved_lse, grad_out, attn_out, w_key, w_value):
    tokens, grad, out, lse = tokens[0], grad_out[0], attn_out[0], saved_lse[0]
    shard, width = tokens.shape
    latents, rows = queries.shape[0], grad.shape[0]
    chips, groups, windows = lax.axis_size("x"), lax.axis_size("z"), lax.axis_size("y")
    heads = lse.shape[1]
    core, chip, group = (lax.axis_index(at).astype(jnp.int32) for at in ("c", "x", "z"))
    head = (2 * chip + core).reshape(1)
    spot = jnp.stack([lax.rem(group, 2), core])
    core, chip, group = core.reshape(1), chip.reshape(1), group.reshape(1)
    tokens, head, core, chip, group, spot = lax.optimization_barrier(
        (tokens, head, core, chip, group, spot)
    )
    sent = pl.pallas_call(
        pack_kernel,
        out_shape=pltpu.HBM((chips, shard + 2 * rows, width), BF16),
        in_specs=[HBM] * 6,
        out_specs=HBM,
        scratch_shapes=[pltpu.SMEM(counts.shape, counts.dtype)]
        + [pltpu.VMEM(ref.shape, ref.dtype) for ref in (tokens, occupancy, grad, out, lse)]
        + [pltpu.VMEM((shard, width), BF16), pltpu.VMEM((chips, 2 * rows, width), BF16)]
        + [pltpu.SemaphoreType.DMA((6,)), pltpu.SemaphoreType.DMA((2, chips))],
        compiler_params=params(60),
    )(counts, tokens, occupancy, grad, out, lse)
    got = swap(sent, "x")
    other = sibling(got)
    grads = pl.pallas_call(
        turn_kernel,
        out_shape=shape((2 * groups, (chips + 1) * rows, HEAD)),
        in_specs=[SMEM, VMEM],
        out_specs=VMEM,
        compiler_params=params(8),
    )(spot, got)
    grads = swap(grads, ("z", "c"))

    back = (chips, shard, width)
    part = (groups * windows, ROWS, width)
    many = (2 * chips * shard, width)
    keep, give, parts = pl.pallas_call(
        main_kernel,
        out_shape=(shape(back), shape(back), shape(part)),
        in_specs=[SMEM] + [VMEM] * 6,
        out_specs=(VMEM,) * 3,
        scratch_shapes=[pltpu.VMEM((HEAD, latents), F32)] + [pltpu.VMEM(many, BF16)] * 2,
        compiler_params=params(40),
    )(head, got, other, grads, queries, w_key, w_value)
    kept, given = pl.pallas_call(
        share_kernel,
        out_shape=(shape(back, F32), shape(back)),
        in_specs=[SMEM] + [VMEM] * 4,
        out_specs=(VMEM,) * 2,
        compiler_params=params(16),
        cost_estimate=pl.CostEstimate(flops=270000000, bytes_accessed=3000000, transcendentals=0),
    )(head, keep, give, w_key, w_value)
    shares = pl.pallas_call(
        combine_kernel,
        out_shape=(shape((shard, width)),) * chips,
        in_specs=[SMEM] + [VMEM] * 2,
        out_specs=(VMEM,) * chips,
        compiler_params=params(16),
    )(chip, kept, sibling(given))
    shares = [shares[0]] + [
        lax.ppermute(shares[ahead], "x", [(at, (at + ahead) % chips) for at in range(chips)])
        for ahead in (2, 1, 3)
    ]
    parts = swap(parts, ("y", "z"))
    parts = pl.pallas_call(
        spread_kernel,
        out_shape=shape(part),
        in_specs=[VMEM],
        out_specs=VMEM,
        compiler_params=params(8),
    )(parts)
    parts = swap(parts, ("y", "z"))
    last = (chips, width + 2 * rows, width)
    sent = pl.pallas_call(
        gather_kernel,
        out_shape=shape(last),
        in_specs=[SMEM, VMEM],
        out_specs=VMEM,
        compiler_params=params(16),
    )(group, parts)
    sent, *shares = lax.optimization_barrier((sent, *shares))
    got = swap(sent, "x")
    other = sibling(got)
    total = pltpu.HBM((width, heads * HEAD), F32)
    staging = [
        pltpu.VMEM((chips, 2, width, HEAD), F32),
        pltpu.SemaphoreType.DMA((chips, 2)),
    ]
    grad_tokens, key_total, value_total = pl.pallas_call(
        tokens_kernel,
        out_shape=(shape((shard, width)), total, total),
        in_specs=[SMEM] * 2 + [VMEM] * (chips + 3),
        out_specs=(VMEM, HBM, HBM),
        scratch_shapes=staging,
        compiler_params=params(16),
        cost_estimate=pl.CostEstimate(flops=2000000, bytes_accessed=3000000, transcendentals=256),
    )(core, counts, got, *shares, tokens, occupancy)
    query_rows, key_total, value_total = pl.pallas_call(
        finish_kernel,
        out_shape=(shape((rows, heads * HEAD), F32), total, total),
        in_specs=[SMEM] + [VMEM] * 2 + [HBM] * 2,
        out_specs=(VMEM, HBM, HBM),
        input_output_aliases={3: 1, 4: 2},
        scratch_shapes=staging,
        compiler_params=params(16),
    )(core, got, other, key_total, value_total)
    return grad_tokens[None], query_rows, key_total, value_total


def solution(mesh):
    seq, dp = mesh.shape["seq"], mesh.shape["dp"]
    split = Mesh(mesh.devices.reshape(seq // 8, 4, 2, dp), ("z", "x", "c", "y"))
    both = ("z", "x", "c")
    rows = P("y", both, None)
    return jax.shard_map(
        body,
        mesh=split,
        in_specs=(rows, P("y", both), P("y", both), P(), rows, rows, rows, P(), P()),
        out_specs=(rows, P(both, None), P(), P()),
        check_vma=False,
    )
```
